32 devices in a mesh: chain: 2 (over y), tm: 4 (over z), src: 2 (over x), col: 2 (over core).
Axes of the slice: x: 2, y: 2, z: 4, core: 2. Of those that a mesh axis runs over, the one named last changes fastest.
Arguments:
- cluster_maps: bfloat16 [4, 2048, 1024], P('tm', 'chain'), parts along dimension 1, may hold values from -2 to 2
- inverse_maps: bfloat16 [4, 2048, 1024], P('tm', 'chain'), parts along dimension 1, may hold values from -2 to 2
- seed_columns: float32 [4, 64, 2048], P('tm', ('src', 'col'), 'chain'), parts along dimension 2, may hold values from -1 to 1, as said below
- seed_rows: float32 [4, 64, 2048], P('tm', ('src', 'col'), 'chain'), parts along dimension 2, may hold values from -1 to 1
- ising_field: int32 [4, 4, 1024], P('tm', 'chain'), parts along dimension 1, may hold values 0 or 1
- hop_bonds: int32 [2, 1024], replicated, may hold values 0 or 1
Outputs:
- correlator: float32 [4, 64, 2048], P('tm', ('src', 'col'), 'chain'), parts along dimension 2
The draws below stay inside these ranges and needn't reach their ends.
There are 2 independent parts, one for each index of `chain`. The reference program is written for one: setup_inputs(seed, part) draws one part's arguments, and reference() takes and returns one part's arrays. A program takes and returns all parts, laid end to end along the dimension named above; an argument that names none is the same for every part. Nothing has to cross between parts.
Inputs may be any that keep to these rules, and one draw needn't show every extreme that they name: Rows of seed_columns and seed_rows come from one equal-time Green block per cluster.
All inputs are finite; a program needn't handle non-finite values. No bound on the sum of `ising_field` on one device may be relied on, other than what follows from the above.
Results may differ from the reference program's by a relative error of at most 0.012.
The reference program's roundings to bfloat16 on the way count: a program that leaves them out, or rounds other values in their place, can miss the bound.
Values may be sent and summed in bfloat16 or wider, within the bound.
No kernel may reach another device: no remote copies, remote signals or barrier semaphores. Data moves between devices by JAX's collectives and lax.ppermute only.
A program may use at most 64 MiB of HBM per device.

```python
import math
import jax
import jax.numpy as jnp
from jax import lax

SIDE = 32
SITES = 1024
WRAPS = 2
REFS = 64
CLUSTERS = 4


def map_noise(key):
    noise_key = jax.random.fold_in(key, 11)
    shape_full = (CLUSTERS, SITES, SITES)
    noise_field = jnp.clip(jax.random.normal(noise_key, shape_full, jnp.float32), -4.0, 4.0)
    return noise_field * (0.25 / SIDE)


def draw_cluster_maps(key, part):
    noise_field = map_noise(key)
    identity = jnp.eye(SITES, dtype=jnp.float32)[None]
    return (identity + noise_field).astype(jnp.bfloat16)


def draw_inverse_maps(key, part):
    noise_field = map_noise(key)
    identity = jnp.eye(SITES, dtype=jnp.float32)[None]
    squared = jnp.einsum('cij,cjk->cik', noise_field, noise_field, precision=lax.Precision.HIGHEST)
    cubic_term = jnp.einsum('cij,cjk->cik', squared, noise_field, precision=lax.Precision.HIGHEST)
    return (identity - noise_field + squared - cubic_term).astype(jnp.bfloat16)


def green_seed(key):
    seed_key = jax.random.fold_in(key, 23)
    shape_full = (CLUSTERS, SITES, SITES)
    values = jnp.clip(jax.random.normal(seed_key, shape_full, jnp.float32), -4.0, 4.0)
    return values * (1.5 / SIDE)


def draw_seed_columns(key, part):
    return jnp.transpose(green_seed(key)[:, :, :REFS], (0, 2, 1))


def draw_seed_rows(key, part):
    return green_seed(key)[:, :REFS, :]


def with_ends(array, key, low, largest):
    dims = array.shape
    place = [jax.random.randint(jax.random.fold_in(key, axis), (), 0, dims[axis]) for axis in range(len(dims))]
    array = array.at[tuple(place)].set(low)
    longest = dims.index(max(dims))
    place[longest] = (place[longest] + 1) % dims[longest]
    return array.at[tuple(place)].set(largest)


def setup_inputs(seed: int = 0, part: int = 0) -> dict:
    seeds = jax.random.split(jax.random.key(seed), 7)
    own_keys = jax.random.split(jax.random.fold_in(seeds[6], part), 7)
    return {
        "cluster_maps": draw_cluster_maps(jax.random.fold_in(jax.random.fold_in(seeds[6], part), 71), part),
        "inverse_maps": draw_inverse_maps(jax.random.fold_in(jax.random.fold_in(seeds[6], part), 71), part),
        "seed_columns": draw_seed_columns(jax.random.fold_in(jax.random.fold_in(seeds[6], part), 71), part),
        "seed_rows": draw_seed_rows(jax.random.fold_in(jax.random.fold_in(seeds[6], part), 71), part),
        "ising_field": with_ends((jax.random.randint(own_keys[4], (CLUSTERS, WRAPS, SITES), 0, 2) < 1).astype(jnp.int32), jax.random.fold_in(own_keys[4], 1), 0, 1),
        "hop_bonds": with_ends((jax.random.randint(seeds[5], (2, SITES), 0, 4) < 3).astype(jnp.int32), jax.random.fold_in(seeds[5], 1), 0, 1),
    }


time_step = 0.25
field_coupling = math.log(math.exp(0.5) + math.sqrt(math.exp(1.0) - 1.0))

def shifted(values, last_column, first_column):
    ahead_rows = jnp.roll(values, -SIDE, axis=-1)
    behind_rows = jnp.roll(values, SIDE, axis=-1)
    ahead_columns = jnp.where(last_column, jnp.roll(values, SIDE - 1, axis=-1), jnp.roll(values, -1, axis=-1))
    behind_columns = jnp.where(first_column, jnp.roll(values, 1 - SIDE, axis=-1), jnp.roll(values, 1, axis=-1))
    return (ahead_rows, behind_rows, ahead_columns, behind_columns)

def couplings(hop_bonds):
    bonds_float = hop_bonds.astype(jnp.float32)
    positions = jnp.arange(hop_bonds.shape[-1]) % SIDE
    last_column = positions == SIDE - 1
    first_column = positions == 0
    row_bonds = bonds_float[0]
    column_bonds = bonds_float[1]
    row_back = jnp.roll(row_bonds, SIDE)
    column_back = jnp.where(first_column, jnp.roll(column_bonds, 1 - SIDE), jnp.roll(column_bonds, 1))
    return (row_bonds, row_back, column_bonds, column_back, last_column, first_column)

def hopping(values, lattice):
    row_bonds, row_back, column_bonds, column_back, last_column, first_column = lattice
    ahead_rows, behind_rows, ahead_columns, behind_columns = shifted(values, last_column, first_column)
    return -(row_bonds * ahead_rows + row_back * behind_rows + column_bonds * ahead_columns + column_back * behind_columns)

def series(values, lattice, orientation):
    single_hop = hopping(values, lattice)
    double_hop = hopping(single_hop, lattice)
    return values + orientation * time_step * single_hop + 0.5 * time_step * time_step * double_hop

def wrapped_product(forward, partner, spin_values, lattice):
    for wrap_index in range(spin_values.shape[0]):
        scale_up = jnp.exp(field_coupling * spin_values[wrap_index])
        scale_down = jnp.exp(-field_coupling * spin_values[wrap_index])
        forward = series(forward * scale_up, lattice, -1.0)
        partner = series(partner * scale_down, lattice, 1.0)
    return forward * partner

def reference(cluster_maps, inverse_maps, seed_columns, seed_rows, ising_field, hop_bonds):
    clusters = cluster_maps.shape[0]
    lattice = couplings(hop_bonds)
    spin_values = (2 * ising_field - 1).astype(jnp.float32)
    site_ids = jnp.arange(SITES)
    ref_ids = jnp.arange(REFS)
    same_site = (site_ids[None, :] == ref_ids[:, None]).astype(jnp.float32)
    unequal = 1.0 - same_site
    forward = seed_columns
    partner = seed_rows - same_site[None]
    results = []
    for displacement in range(clusters):
        if displacement > 0:
            maps_here = jnp.roll(cluster_maps, -displacement, axis=0).astype(jnp.float32)
            inverse_here = jnp.roll(inverse_maps, -displacement, axis=0).astype(jnp.float32)
            forward_low = lax.optimization_barrier(forward.astype(jnp.bfloat16)).astype(jnp.float32)
            partner_low = lax.optimization_barrier(partner.astype(jnp.bfloat16)).astype(jnp.float32)
            forward = jnp.einsum('lri,lmi->lrm', forward_low, maps_here)
            partner = jnp.einsum('lri,lim->lrm', partner_low, inverse_here)
        spins_here = jnp.moveaxis(jnp.roll(spin_values, -displacement, axis=0), 1, 0)[:, :, None, :]
        product = wrapped_product(forward, partner, spins_here, lattice)
        results.append(lax.optimization_barrier(jnp.sum(product, axis=0)) * unequal)
    return jnp.stack(results) * (SITES / clusters)
```

```python
import functools
import math

import jax
import jax.numpy as jnp
from jax import lax
from jax.experimental import pallas as pl
from jax.experimental.pallas import tpu as pltpu
from jax.sharding import PartitionSpec as P

time_step = 0.25
field_coupling = math.log(math.exp(0.5) + math.sqrt(math.exp(1.0) - 1.0))

LANES = 128


def rolled(blocks, shift):
    return [pltpu.roll(block, shift % LANES, 1) for block in blocks]


def hops(blocks, side, coefs):
    count = len(blocks)
    lane = lax.broadcasted_iota(jnp.int32, blocks[0].shape, 1)
    column = lane % side
    ahead = rolled(blocks, -side)
    behind = rolled(blocks, side)
    right, right_wrap = rolled(blocks, -1), rolled(blocks, side - 1)
    left, left_wrap = rolled(blocks, 1), rolled(blocks, 1 - side)
    out = []
    for j in range(count):
        row_ahead = jnp.where(lane < LANES - side, ahead[j], ahead[(j + 1) % count])
        row_behind = jnp.where(lane >= side, behind[j], behind[j - 1])
        column_ahead = jnp.where(column == side - 1, right_wrap[j], right[j])
        column_behind = jnp.where(column == 0, left_wrap[j], left[j])
        up, down, forth, back = [c[j] for c in coefs]
        out.append(up * row_ahead + down * row_behind + (forth * column_ahead + back * column_behind))
    return out


def series(blocks, side, coefs, sign):
    inner = [u + (0.5 * sign) * h for u, h in zip(blocks, hops(blocks, side, coefs))]
    return [u + sign * h for u, h in zip(blocks, hops(inner, side, coefs))]


def split(values):
    return [values[:, j : j + LANES] for j in range(0, values.shape[1], LANES)]


def coupling_blocks(bonds, side):
    weights = bonds.astype(jnp.float32) * time_step
    rows, columns = split(weights[0:1]), split(weights[1:2])
    count = len(rows)
    lane = lax.broadcasted_iota(jnp.int32, rows[0].shape, 1)
    moved = rolled(rows, side)
    rows_back = [jnp.where(lane >= side, moved[j], moved[j - 1]) for j in range(count)]
    columns_back = [
        jnp.where(lane % side == 0, wrap, left)
        for wrap, left in zip(rolled(columns, 1 - side), rolled(columns, 1))
    ]
    return rows, rows_back, columns, columns_back


def measure_kernel(side, base_ref, forward_ref, partner_ref, field_ref, bonds_ref, out_ref):
    coefs = coupling_blocks(bonds_ref[...], side)
    spins = (2 * field_ref[...] - 1).astype(jnp.float32)
    up, down = jnp.exp(field_coupling * spins), jnp.exp(-field_coupling * spins)
    forward, partner = split(forward_ref[...]), split(partner_ref[...])
    for wrap in range(spins.shape[0]):
        scale_up, scale_down = split(up[wrap : wrap + 1]), split(down[wrap : wrap + 1])
        forward = series([u * s for u, s in zip(forward, scale_up)], side, coefs, 1.0)
        partner = series([u * s for u, s in zip(partner, scale_down)], side, coefs, -1.0)
    row = lax.broadcasted_iota(jnp.int32, forward[0].shape, 0) + base_ref[0]
    lane = lax.broadcasted_iota(jnp.int32, forward[0].shape, 1)
    for j, (f, p) in enumerate(zip(forward, partner)):
        term = jnp.where(lane + j * LANES == row, 0.0, f * p)
        out_ref[:, j * LANES : (j + 1) * LANES] = term.astype(out_ref.dtype)


def measured(base, forward, partner, field, bonds):
    vmem = pl.BlockSpec(memory_space=pltpu.VMEM)
    side = math.isqrt(bonds.shape[1])
    return pl.pallas_call(
        functools.partial(measure_kernel, side),
        out_shape=jax.ShapeDtypeStruct(forward.shape, jnp.bfloat16),
        in_specs=[pl.BlockSpec(memory_space=pltpu.SMEM), vmem, vmem, vmem, vmem],
        out_specs=vmem,
        cost_estimate=pl.CostEstimate(flops=200 * forward.size, bytes_accessed=8 * forward.size, transcendentals=0),
    )(base, forward, partner, field, bonds)


def per_device(cluster_maps, inverse_maps, seed_columns, seed_rows, ising_field, hop_bonds):
    clusters = lax.axis_size("tm")
    anchor = lax.axis_index("tm")
    ref_rows, sites = seed_columns.shape[1:]
    base = lax.axis_index(("src", "col")) * ref_rows
    same_site = jnp.arange(sites)[None, :] == (base + jnp.arange(ref_rows))[:, None]
    forward_map, inverse_map = cluster_maps[0], inverse_maps[0]
    forward = seed_columns[0]
    partner = seed_rows[0] - same_site.astype(jnp.float32)
    around = [(i, (i + 1) % clusters) for i in range(clusters)]

    def measure(forward_block, partner_block):
        return measured(base[None].astype(jnp.int32), forward_block, partner_block, ising_field[0], hop_bonds)

    terms = []
    for displacement in range(clusters):
        if displacement:
            forward_low = lax.ppermute(forward.astype(jnp.bfloat16), "tm", around)
            partner_low = lax.ppermute(partner.astype(jnp.bfloat16), "tm", around)
            forward = lax.dot_general(
                forward_low, forward_map, (((1,), (1,)), ((), ())), preferred_element_type=jnp.float32
            )
            partner = jnp.dot(partner_low, inverse_map, preferred_element_type=jnp.float32)
        terms.append(measure(forward, partner))
    terms = jnp.stack(terms)
    total = None
    for step in range(clusters):
        term = lax.dynamic_index_in_dim(terms, (anchor + step) % clusters, 0, keepdims=False)
        if step:
            term = lax.ppermute(term, "tm", [(i, (i + step) % clusters) for i in range(clusters)])
        total = term.astype(jnp.float32) if total is None else total + term.astype(jnp.float32)
    return (total * (sites / clusters))[None]


def solution(mesh):
    in_specs = (
        P("tm", "chain", None),
        P("tm", "chain", None),
        P("tm", ("src", "col"), "chain"),
        P("tm", ("src", "col"), "chain"),
        P("tm", "chain", None),
        P(),
    )
    out_specs = P("tm", ("src", "col"), "chain")
    return jax.shard_map(
        per_device, mesh=mesh, in_specs=in_specs, out_specs=out_specs, check_vma=False
    )
```

```python
import functools
import math

import jax
import jax.numpy as jnp
from jax import lax
from jax.experimental import pallas as pl
from jax.experimental.pallas import tpu as pltpu
from jax.sharding import PartitionSpec as P

time_step = 0.25
field_coupling = math.log(math.exp(0.5) + math.sqrt(math.exp(1.0) - 1.0))

LANES = 128


def rolled(blocks, shift):
    return [pltpu.roll(block, shift % LANES, 1) for block in blocks]


def hops(blocks, side, coefs):
    count = len(blocks)
    lane = lax.broadcasted_iota(jnp.int32, blocks[0].shape, 1)
    column = lane % side
    ahead = rolled(blocks, -side)
    behind = rolled(blocks, side)
    right, right_wrap = rolled(blocks, -1), rolled(blocks, side - 1)
    left, left_wrap = rolled(blocks, 1), rolled(blocks, 1 - side)
    out = []
    for j in range(count):
        row_ahead = jnp.where(lane < LANES - side, ahead[j], ahead[(j + 1) % count])
        row_behind = jnp.where(lane >= side, behind[j], behind[j - 1])
        column_ahead = jnp.where(column == side - 1, right_wrap[j], right[j])
        column_behind = jnp.where(column == 0, left_wrap[j], left[j])
        up, down, forth, back = [c[j] for c in coefs]
        out.append(up * row_ahead + down * row_behind + (forth * column_ahead + back * column_behind))
    return out


def series(blocks, side, coefs, sign):
    inner = [u + (0.5 * sign) * h for u, h in zip(blocks, hops(blocks, side, coefs))]
    return [u + sign * h for u, h in zip(blocks, hops(inner, side, coefs))]


def split(values):
    return [values[:, j : j + LANES] for j in range(0, values.shape[1], LANES)]


def coupling_blocks(bonds, side):
    weights = bonds.astype(jnp.float32) * time_step
    rows, columns = split(weights[0:1]), split(weights[1:2])
    count = len(rows)
    lane = lax.broadcasted_iota(jnp.int32, rows[0].shape, 1)
    moved = rolled(rows, side)
    rows_back = [jnp.where(lane >= side, moved[j], moved[j - 1]) for j in range(count)]
    columns_back = [
        jnp.where(lane % side == 0, wrap, left)
        for wrap, left in zip(rolled(columns, 1 - side), rolled(columns, 1))
    ]
    return rows, rows_back, columns, columns_back


def measure_kernel(side, base_ref, forward_ref, partner_ref, field_ref, bonds_ref, out_ref):
    coefs = coupling_blocks(bonds_ref[...], side)
    spins = (2 * field_ref[...] - 1).astype(jnp.float32)
    up, down = jnp.exp(field_coupling * spins), jnp.exp(-field_coupling * spins)
    forward, partner = split(forward_ref[...]), split(partner_ref[...])
    for wrap in range(spins.shape[0]):
        scale_up, scale_down = split(up[wrap : wrap + 1]), split(down[wrap : wrap + 1])
        forward = series([u * s for u, s in zip(forward, scale_up)], side, coefs, 1.0)
        partner = series([u * s for u, s in zip(partner, scale_down)], side, coefs, -1.0)
    row = lax.broadcasted_iota(jnp.int32, forward[0].shape, 0) + base_ref[0]
    lane = lax.broadcasted_iota(jnp.int32, forward[0].shape, 1)
    for j, (f, p) in enumerate(zip(forward, partner)):
        term = jnp.where(lane + j * LANES == row, 0.0, f * p)
        out_ref[:, j * LANES : (j + 1) * LANES] = term.astype(out_ref.dtype)


def measured(base, forward, partner, field, bonds):
    vmem = pl.BlockSpec(memory_space=pltpu.VMEM)
    side = math.isqrt(bonds.shape[1])
    return pl.pallas_call(
        functools.partial(measure_kernel, side),
        out_shape=jax.ShapeDtypeStruct(forward.shape, jnp.bfloat16),
        in_specs=[pl.BlockSpec(memory_space=pltpu.SMEM), vmem, vmem, vmem, vmem],
        out_specs=vmem,
        compiler_params=pltpu.CompilerParams(vmem_limit_bytes=4 << 20),
        cost_estimate=pl.CostEstimate(flops=200 * forward.size, bytes_accessed=8 * forward.size, transcendentals=0),
    )(base, forward, partner, field, bonds)


def per_device(cluster_maps, inverse_maps, seed_columns, seed_rows, ising_field, hop_bonds):
    clusters = lax.axis_size("tm")
    anchor = lax.axis_index("tm")
    ref_rows, sites = seed_columns.shape[1:]
    base = lax.axis_index(("src", "col")) * ref_rows
    same_site = jnp.arange(sites)[None, :] == (base + jnp.arange(ref_rows))[:, None]
    forward_map, inverse_map = cluster_maps[0], inverse_maps[0]
    forward = seed_columns[0]
    partner = seed_rows[0] - same_site.astype(jnp.float32)
    around = [(i, (i + 1) % clusters) for i in range(clusters)]

    def measure(forward_block, partner_block):
        return measured(base[None].astype(jnp.int32), forward_block, partner_block, ising_field[0], hop_bonds)

    terms = []
    for displacement in range(clusters):
        if displacement:
            low = jnp.concatenate([forward.astype(jnp.bfloat16), partner.astype(jnp.bfloat16)])
            low = lax.ppermute(low, "tm", around)
            forward = lax.dot_general(
                low[:ref_rows], forward_map, (((1,), (1,)), ((), ())), preferred_element_type=jnp.float32
            )
            partner = jnp.dot(low[ref_rows:], inverse_map, preferred_element_type=jnp.float32)
        terms.append(measure(forward, partner))
    terms = jnp.stack(terms)
    total = None
    for step in (0,1,2,3):
        place = anchor ^ step
        term = lax.dynamic_index_in_dim(terms, place, 0, keepdims=False)
        if step:
            term = lax.ppermute(term, "tm", [(i, i ^ step) for i in range(clusters)])
        total = term.astype(jnp.float32) if total is None else total + term.astype(jnp.float32)
    return (total * (sites / clusters))[None]


def solution(mesh):
    in_specs = (
        P("tm", "chain", None),
        P("tm", "chain", None),
        P("tm", ("src", "col"), "chain"),
        P("tm", ("src", "col"), "chain"),
        P("tm", "chain", None),
        P(),
    )
    out_specs = P("tm", ("src", "col"), "chain")
    return jax.shard_map(
        per_device, mesh=mesh, in_specs=in_specs, out_specs=out_specs, check_vma=False
    )
```

```python
import functools
import math

import jax
import jax.numpy as jnp
from jax import lax
from jax.experimental import pallas as pl
from jax.experimental.pallas import tpu as pltpu
from jax.sharding import PartitionSpec as P

time_step = 0.25
field_coupling = math.log(math.exp(0.5) + math.sqrt(math.exp(1.0) - 1.0))

LANES = 128
VMEM = pl.BlockSpec(memory_space=pltpu.VMEM)
SMEM = pl.BlockSpec(memory_space=pltpu.SMEM)
ANY = pl.BlockSpec(memory_space=pl.ANY)


def params(mebibytes=4):
    return pltpu.CompilerParams(vmem_limit_bytes=mebibytes << 20)


def cost(flops, bytes_accessed):
    return pl.CostEstimate(flops=flops, bytes_accessed=bytes_accessed, transcendentals=0)


def rolled(blocks, shift):
    return [pltpu.roll(block, shift % LANES, 1) for block in blocks]


def split(values):
    return [values[:, j : j + LANES] for j in range(0, values.shape[1], LANES)]


def hops(blocks, side, coefs):
    count = len(blocks)
    lane = lax.broadcasted_iota(jnp.int32, blocks[0].shape, 1)
    column = lane % side
    ahead = rolled(blocks, -side)
    behind = rolled(blocks, side)
    right, right_wrap = rolled(blocks, -1), rolled(blocks, side - 1)
    left, left_wrap = rolled(blocks, 1), rolled(blocks, 1 - side)
    out = []
    for j in range(count):
        row_ahead = jnp.where(lane < LANES - side, ahead[j], ahead[(j + 1) % count])
        row_behind = jnp.where(lane >= side, behind[j], behind[j - 1])
        column_ahead = jnp.where(column == side - 1, right_wrap[j], right[j])
        column_behind = jnp.where(column == 0, left_wrap[j], left[j])
        up, down, forth, back = [c[j] for c in coefs]
        out.append((up * row_ahead + down * row_behind) + (forth * column_ahead + back * column_behind))
    return out


def factors_kernel(side, field_ref, bonds_ref, out_ref):
    weights = bonds_ref[...].astype(jnp.float32) * time_step
    rows, columns = split(weights[0:1]), split(weights[1:2])
    lane = lax.broadcasted_iota(jnp.int32, rows[0].shape, 1)
    moved = rolled(rows, side)
    wrapped, left = rolled(columns, 1 - side), rolled(columns, 1)
    for j in range(len(rows)):
        place = slice(j * LANES, (j + 1) * LANES)
        out_ref[0:1, place] = rows[j]
        out_ref[1:2, place] = jnp.where(lane >= side, moved[j], moved[j - 1])
        out_ref[2:3, place] = columns[j]
        out_ref[3:4, place] = jnp.where(lane % side == 0, wrapped[j], left[j])
    spins = (2 * field_ref[...] - 1).astype(jnp.float32)
    wraps = spins.shape[0]
    out_ref[4 : 4 + wraps, :] = jnp.exp(field_coupling * spins)
    out_ref[4 + wraps : 4 + 2 * wraps, :] = jnp.exp(-field_coupling * spins)


def factors(field, bonds):
    wraps, sites = field.shape
    return pl.pallas_call(
        functools.partial(factors_kernel, math.isqrt(sites)),
        out_shape=jax.ShapeDtypeStruct((4 + 2 * wraps, sites), jnp.float32),
        in_specs=[VMEM, VMEM],
        out_specs=VMEM,
        compiler_params=params(),
        cost_estimate=cost(64 * sites, 64 * sites),
    )(field, bonds)


def measure_kernel(side, base_ref, forward_ref, partner_ref, factors_ref, out_ref):
    coefs = [split(factors_ref[k : k + 1, :]) for k in range(4)]
    wraps = (factors_ref.shape[0] - 4) // 2
    forward, partner = split(forward_ref[...]), split(partner_ref[...])
    for wrap in range(wraps):
        scale_up = split(factors_ref[4 + wrap : 5 + wrap, :])
        scale_down = split(factors_ref[4 + wraps + wrap : 5 + wraps + wrap, :])
        forward = [u * s for u, s in zip(forward, scale_up)]
        partner = [u * s for u, s in zip(partner, scale_down)]
        hop_forward, hop_partner = hops(forward, side, coefs), hops(partner, side, coefs)
        half_forward = [u + 0.5 * h for u, h in zip(forward, hop_forward)]
        half_partner = [u - 0.5 * h for u, h in zip(partner, hop_partner)]
        hop_forward, hop_partner = hops(half_forward, side, coefs), hops(half_partner, side, coefs)
        forward = [u + h for u, h in zip(forward, hop_forward)]
        partner = [u - h for u, h in zip(partner, hop_partner)]
    row = lax.broadcasted_iota(jnp.int32, forward[0].shape, 0) + base_ref[0]
    lane = lax.broadcasted_iota(jnp.int32, forward[0].shape, 1)
    for j, (f, p) in enumerate(zip(forward, partner)):
        term = jnp.where(lane + j * LANES == row, 0.0, f * p)
        out_ref[:, j * LANES : (j + 1) * LANES] = term.astype(out_ref.dtype)


def measured(base, forward, partner, rates):
    return pl.pallas_call(
        functools.partial(measure_kernel, math.isqrt(forward.shape[1])),
        out_shape=jax.ShapeDtypeStruct(forward.shape, jnp.bfloat16),
        in_specs=[SMEM, VMEM, VMEM, VMEM],
        out_specs=VMEM,
        compiler_params=params(),
        cost_estimate=cost(200 * forward.size, 12 * forward.size),
    )(base, forward, partner, rates)


def packed_kernel(base_ref, columns_ref, rows_ref, out_ref, columns, rows, arrived):
    copies = [
        pltpu.make_async_copy(columns_ref, columns, arrived.at[0]),
        pltpu.make_async_copy(rows_ref, rows, arrived.at[1]),
    ]
    for copy in copies:
        copy.start()
    for copy in copies:
        copy.wait()
    count = columns.shape[0]
    row = lax.broadcasted_iota(jnp.int32, rows.shape, 0) + base_ref[0]
    lane = lax.broadcasted_iota(jnp.int32, rows.shape, 1)
    out_ref[0:count, :] = columns[...].astype(out_ref.dtype)
    out_ref[count:, :] = jnp.where(lane == row, rows[...] - 1.0, rows[...]).astype(out_ref.dtype)


def packed(base, columns, rows):
    count, sites = columns.shape
    return pl.pallas_call(
        packed_kernel,
        out_shape=jax.ShapeDtypeStruct((2 * count, sites), jnp.bfloat16),
        in_specs=[SMEM, ANY, ANY],
        out_specs=VMEM,
        scratch_shapes=[
            pltpu.VMEM(columns.shape, columns.dtype),
            pltpu.VMEM(rows.shape, rows.dtype),
            pltpu.SemaphoreType.DMA((2,)),
        ],
        compiler_params=params(),
        cost_estimate=cost(4 * rows.size, 12 * rows.size),
    )(
        base,
        pltpu.with_memory_space_constraint(columns, pltpu.HBM),
        pltpu.with_memory_space_constraint(rows, pltpu.HBM),
    )


def turned_kernel(map_ref, out_ref):
    out_ref[...] = map_ref[...].T


def turned(dense):
    return pl.pallas_call(
        turned_kernel,
        out_shape=jax.ShapeDtypeStruct(dense.shape[::-1], dense.dtype),
        in_specs=[VMEM],
        out_specs=VMEM,
        compiler_params=params(8),
        cost_estimate=cost(dense.size, 4 * dense.size),
    )(dense)


def per_device(cluster_maps, inverse_maps, seed_columns, seed_rows, ising_field, hop_bonds):
    clusters = lax.axis_size("tm")
    anchor = lax.axis_index("tm")
    ref_rows, sites = seed_columns.shape[1:]
    first = lax.axis_index(("src", "col")) * ref_rows
    base = first[None].astype(jnp.int32)
    same_site = jnp.arange(sites)[None, :] == (first + jnp.arange(ref_rows))[:, None]
    around = [(i, (i + 1) % clusters) for i in range(clusters)]
    forward_map, inverse_map = cluster_maps[0], inverse_maps[0]
    forward = seed_columns[0]
    partner = seed_rows[0] - same_site.astype(jnp.float32)
    rates = factors(ising_field[0], hop_bonds)

    terms = [measured(base, forward, partner, rates)]
    low = packed(base, seed_columns[0], seed_rows[0])
    for displacement in range(1, clusters):
        if displacement >= 3:
            low, *terms[: displacement - 1] = lax.optimization_barrier((low, *terms[: displacement - 1]))
        low = lax.ppermute(low, "tm", around)
        forward = lax.dot_general(
            low[:ref_rows], forward_map, (((1,), (1,)), ((), ())), preferred_element_type=jnp.float32
        )
        partner = jnp.dot(low[ref_rows:], inverse_map, preferred_element_type=jnp.float32)
        terms.append(measured(base, forward, partner, rates))
        low = jnp.concatenate([forward, partner]).astype(jnp.bfloat16)
    terms = jnp.stack(terms)
    total = None
    for step in (0, 2, 1, 3):
        term = lax.dynamic_index_in_dim(terms, anchor ^ step, 0, keepdims=False)
        if step:
            term = lax.ppermute(term, "tm", [(i, i ^ step) for i in range(clusters)])
        total = term.astype(jnp.float32) if total is None else total + term.astype(jnp.float32)
    return (total * (sites / clusters))[None]


def solution(mesh):
    in_specs = (
        P("tm", "chain", None),
        P("tm", "chain", None),
        P("tm", ("src", "col"), "chain"),
        P("tm", ("src", "col"), "chain"),
        P("tm", "chain", None),
        P(),
    )
    out_specs = P("tm", ("src", "col"), "chain")
    return jax.shard_map(
        per_device, mesh=mesh, in_specs=in_specs, out_specs=out_specs, check_vma=False
    )
```

```python
import functools
import math

import jax
import jax.numpy as jnp
from jax import lax
from jax.experimental import pallas as pl
from jax.experimental.pallas import tpu as pltpu
from jax.sharding import PartitionSpec as P

time_step = 0.25
field_coupling = math.log(math.exp(0.5) + math.sqrt(math.exp(1.0) - 1.0))

LANES = 128
VMEM = pl.BlockSpec(memory_space=pltpu.VMEM)
SMEM = pl.BlockSpec(memory_space=pltpu.SMEM)
ANY = pl.BlockSpec(memory_space=pl.ANY)


def params(mebibytes=4):
    return pltpu.CompilerParams(vmem_limit_bytes=mebibytes << 20)


def cost(flops, bytes_accessed):
    return pl.CostEstimate(flops=flops, bytes_accessed=bytes_accessed, transcendentals=0)


def rolled(blocks, shift):
    return [pltpu.roll(block, shift % LANES, 1) for block in blocks]


def split(values):
    return [values[:, j : j + LANES] for j in range(0, values.shape[1], LANES)]


def hops(blocks, side, coefs):
    count = len(blocks)
    lane = lax.broadcasted_iota(jnp.int32, blocks[0].shape, 1)
    column = lane % side
    ahead = rolled(blocks, -side)
    behind = rolled(blocks, side)
    right, right_wrap = rolled(blocks, -1), rolled(blocks, side - 1)
    left, left_wrap = rolled(blocks, 1), rolled(blocks, 1 - side)
    out = []
    for j in range(count):
        row_ahead = jnp.where(lane < LANES - side, ahead[j], ahead[(j + 1) % count])
        row_behind = jnp.where(lane >= side, behind[j], behind[j - 1])
        column_ahead = jnp.where(column == side - 1, right_wrap[j], right[j])
        column_behind = jnp.where(column == 0, left_wrap[j], left[j])
        up, down, forth, back = [c[j] for c in coefs]
        out.append((up * row_ahead + down * row_behind) + (forth * column_ahead + back * column_behind))
    return out


def factors_kernel(side, field_ref, bonds_ref, out_ref):
    weights = bonds_ref[...].astype(jnp.float32) * time_step
    rows, columns = split(weights[0:1]), split(weights[1:2])
    lane = lax.broadcasted_iota(jnp.int32, rows[0].shape, 1)
    moved = rolled(rows, side)
    wrapped, left = rolled(columns, 1 - side), rolled(columns, 1)
    for j in range(len(rows)):
        place = slice(j * LANES, (j + 1) * LANES)
        out_ref[0:1, place] = rows[j]
        out_ref[1:2, place] = jnp.where(lane >= side, moved[j], moved[j - 1])
        out_ref[2:3, place] = columns[j]
        out_ref[3:4, place] = jnp.where(lane % side == 0, wrapped[j], left[j])
    spins = (2 * field_ref[...] - 1).astype(jnp.float32)
    wraps = spins.shape[0]
    out_ref[4 : 4 + wraps, :] = jnp.exp(field_coupling * spins)
    out_ref[4 + wraps : 4 + 2 * wraps, :] = jnp.exp(-field_coupling * spins)


def factors(field, bonds):
    wraps, sites = field.shape
    return pl.pallas_call(
        functools.partial(factors_kernel, math.isqrt(sites)),
        out_shape=jax.ShapeDtypeStruct((4 + 2 * wraps, sites), jnp.float32),
        in_specs=[VMEM, VMEM],
        out_specs=VMEM,
        compiler_params=params(),
        cost_estimate=cost(64 * sites, 64 * sites),
    )(field, bonds)


def measure_kernel(side, base_ref, forward_ref, partner_ref, factors_ref, *rest):
    out_ref = rest[-1]
    coefs = [split(factors_ref[k : k + 1, :]) for k in range(4)]
    wraps = (factors_ref.shape[0] - 4) // 2
    forward, partner = split(forward_ref[...]), split(partner_ref[...])
    for wrap in range(wraps):
        scale_up = split(factors_ref[4 + wrap : 5 + wrap, :])
        scale_down = split(factors_ref[4 + wraps + wrap : 5 + wraps + wrap, :])
        forward = [u * s for u, s in zip(forward, scale_up)]
        partner = [u * s for u, s in zip(partner, scale_down)]
        hop_forward, hop_partner = hops(forward, side, coefs), hops(partner, side, coefs)
        half_forward = [u + 0.5 * h for u, h in zip(forward, hop_forward)]
        half_partner = [u - 0.5 * h for u, h in zip(partner, hop_partner)]
        hop_forward, hop_partner = hops(half_forward, side, coefs), hops(half_partner, side, coefs)
        forward = [u + h for u, h in zip(forward, hop_forward)]
        partner = [u - h for u, h in zip(partner, hop_partner)]
    row = lax.broadcasted_iota(jnp.int32, forward[0].shape, 0) + base_ref[0]
    lane = lax.broadcasted_iota(jnp.int32, forward[0].shape, 1)
    for j, (f, p) in enumerate(zip(forward, partner)):
        term = jnp.where(lane + j * LANES == row, 0.0, f * p)
        out_ref[:, j * LANES : (j + 1) * LANES] = term.astype(out_ref.dtype)


def measured(base, forward, partner, rates, *kept):
    return pl.pallas_call(
        functools.partial(measure_kernel, math.isqrt(forward.shape[1])),
        out_shape=jax.ShapeDtypeStruct(forward.shape, jnp.bfloat16),
        in_specs=[SMEM, VMEM, VMEM, VMEM] + [ANY] * len(kept),
        out_specs=VMEM,
        compiler_params=params(),
        cost_estimate=cost(200 * forward.size, 12 * forward.size),
    )(base, forward, partner, rates, *(pltpu.with_memory_space_constraint(k, pltpu.VMEM) for k in kept))


def packed_kernel(base_ref, columns_ref, rows_ref, out_ref, columns, rows, arrived):
    copies = [
        pltpu.make_async_copy(columns_ref, columns, arrived.at[0]),
        pltpu.make_async_copy(rows_ref, rows, arrived.at[1]),
    ]
    for copy in copies:
        copy.start()
    for copy in copies:
        copy.wait()
    count = columns.shape[0]
    row = lax.broadcasted_iota(jnp.int32, rows.shape, 0) + base_ref[0]
    lane = lax.broadcasted_iota(jnp.int32, rows.shape, 1)
    out_ref[0:count, :] = columns[...].astype(out_ref.dtype)
    out_ref[count:, :] = jnp.where(lane == row, rows[...] - 1.0, rows[...]).astype(out_ref.dtype)


def packed(base, columns, rows):
    count, sites = columns.shape
    return pl.pallas_call(
        packed_kernel,
        out_shape=jax.ShapeDtypeStruct((2 * count, sites), jnp.bfloat16),
        in_specs=[SMEM, ANY, ANY],
        out_specs=VMEM,
        scratch_shapes=[
            pltpu.VMEM(columns.shape, columns.dtype),
            pltpu.VMEM(rows.shape, rows.dtype),
            pltpu.SemaphoreType.DMA((2,)),
        ],
        compiler_params=params(),
        cost_estimate=cost(4 * rows.size, 12 * rows.size),
    )(
        base,
        pltpu.with_memory_space_constraint(columns, pltpu.HBM),
        pltpu.with_memory_space_constraint(rows, pltpu.HBM),
    )


def turned_kernel(map_ref, out_ref):
    out_ref[...] = map_ref[...].T


def turned(dense):
    return pl.pallas_call(
        turned_kernel,
        out_shape=jax.ShapeDtypeStruct(dense.shape[::-1], dense.dtype),
        in_specs=[VMEM],
        out_specs=VMEM,
        compiler_params=params(8),
        cost_estimate=cost(dense.size, 4 * dense.size),
    )(dense)


def per_device(cluster_maps, inverse_maps, seed_columns, seed_rows, ising_field, hop_bonds):
    clusters = lax.axis_size("tm")
    anchor = lax.axis_index("tm")
    ref_rows, sites = seed_columns.shape[1:]
    cores = lax.axis_size("col")
    core = lax.axis_index("col")

    def first_ref(displacement):
        origin = (core - (displacement > anchor).astype(jnp.int32)) % cores
        return (lax.axis_index("src") * cores + origin) * ref_rows

    def route(targets):
        return [
            (k * cores + c, t * cores + (c + shift) % cores)
            for k, (t, shift) in enumerate(targets)
            for c in range(cores)
        ]

    around = route([((k + 1) % clusters, (k + 1) // clusters) for k in range(clusters)])
    first = first_ref(0)
    same_site = jnp.arange(sites)[None, :] == (first + jnp.arange(ref_rows))[:, None]
    forward_map, inverse_map = turned(cluster_maps[0]), inverse_maps[0]
    forward = seed_columns[0]
    partner = seed_rows[0] - same_site.astype(jnp.float32)
    rates = factors(ising_field[0], hop_bonds)

    terms = [measured(first[None], forward, partner, rates)]
    low = packed(first[None], seed_columns[0], seed_rows[0])
    for displacement in range(1, clusters):
        if displacement >= 3:
            low, *terms[: displacement - 1] = lax.optimization_barrier((low, *terms[: displacement - 1]))
        low = lax.ppermute(low, ("tm", "col"), around)
        forward = lax.dot_general(
            low[:ref_rows], forward_map, (((1,), (0,)), ((), ())), preferred_element_type=jnp.float32
        )
        partner = jnp.dot(low[ref_rows:], inverse_map, preferred_element_type=jnp.float32)
        terms.append(measured(first_ref(displacement)[None], forward, partner, rates, *((forward_map,) if displacement == clusters - 2 else ())))
        low = jnp.concatenate([forward, partner]).astype(jnp.bfloat16)
    terms = jnp.stack(terms)
    total = None
    for step in (0, 2, 1, 3):
        term = lax.dynamic_index_in_dim(terms, anchor ^ step, 0, keepdims=False)
        if step:
            back = route([(k ^ step, -(k < k ^ step)) for k in range(clusters)])
            term = lax.ppermute(term, ("tm", "col"), back)
        total = term.astype(jnp.float32) if total is None else total + term.astype(jnp.float32)
    return (total * (sites / clusters))[None]


def solution(mesh):
    in_specs = (
        P("tm", "chain", None),
        P("tm", "chain", None),
        P("tm", ("src", "col"), "chain"),
        P("tm", ("src", "col"), "chain"),
        P("tm", "chain", None),
        P(),
    )
    out_specs = P("tm", ("src", "col"), "chain")
    return jax.shard_map(
        per_device, mesh=mesh, in_specs=in_specs, out_specs=out_specs, check_vma=False
    )
```

```python
import functools
import math

import jax
import jax.numpy as jnp
from jax import lax
from jax.experimental import pallas as pl
from jax.experimental.pallas import tpu as pltpu
from jax.sharding import PartitionSpec as P

time_step = 0.25
field_coupling = math.log(math.exp(0.5) + math.sqrt(math.exp(1.0) - 1.0))

LANES = 128
VMEM = pl.BlockSpec(memory_space=pltpu.VMEM)
SMEM = pl.BlockSpec(memory_space=pltpu.SMEM)
ANY = pl.BlockSpec(memory_space=pl.ANY)


def params(mebibytes=4):
    return pltpu.CompilerParams(vmem_limit_bytes=mebibytes << 20)


def cost(flops, bytes_accessed):
    return pl.CostEstimate(flops=flops, bytes_accessed=bytes_accessed, transcendentals=0)


def rolled(blocks, shift):
    return [pltpu.roll(block, shift % LANES, 1) for block in blocks]


def split(values):
    return [values[:, j : j + LANES] for j in range(0, values.shape[1], LANES)]


def hops(blocks, side, coefs):
    count = len(blocks)
    lane = lax.broadcasted_iota(jnp.int32, blocks[0].shape, 1)
    column = lane % side
    ahead = rolled(blocks, -side)
    behind = rolled(blocks, side)
    right, right_wrap = rolled(blocks, -1), rolled(blocks, side - 1)
    left, left_wrap = rolled(blocks, 1), rolled(blocks, 1 - side)
    out = []
    for j in range(count):
        row_ahead = jnp.where(lane < LANES - side, ahead[j], ahead[(j + 1) % count])
        row_behind = jnp.where(lane >= side, behind[j], behind[j - 1])
        column_ahead = jnp.where(column == side - 1, right_wrap[j], right[j])
        column_behind = jnp.where(column == 0, left_wrap[j], left[j])
        up, down, forth, back = [c[j] for c in coefs]
        out.append((up * row_ahead + down * row_behind) + (forth * column_ahead + back * column_behind))
    return out


def factors_kernel(side, field_ref, bonds_ref, out_ref):
    weights = bonds_ref[...].astype(jnp.float32) * time_step
    rows, columns = split(weights[0:1]), split(weights[1:2])
    lane = lax.broadcasted_iota(jnp.int32, rows[0].shape, 1)
    moved = rolled(rows, side)
    wrapped, left = rolled(columns, 1 - side), rolled(columns, 1)
    for j in range(len(rows)):
        place = slice(j * LANES, (j + 1) * LANES)
        out_ref[0:1, place] = rows[j]
        out_ref[1:2, place] = jnp.where(lane >= side, moved[j], moved[j - 1])
        out_ref[2:3, place] = columns[j]
        out_ref[3:4, place] = jnp.where(lane % side == 0, wrapped[j], left[j])
    spins = (2 * field_ref[...] - 1).astype(jnp.float32)
    wraps = spins.shape[0]
    out_ref[4 : 4 + wraps, :] = jnp.exp(field_coupling * spins)
    out_ref[4 + wraps : 4 + 2 * wraps, :] = jnp.exp(-field_coupling * spins)


def factors(field, bonds):
    wraps, sites = field.shape
    return pl.pallas_call(
        functools.partial(factors_kernel, math.isqrt(sites)),
        out_shape=jax.ShapeDtypeStruct((4 + 2 * wraps, sites), jnp.float32),
        in_specs=[VMEM, VMEM],
        out_specs=VMEM,
        compiler_params=params(),
        cost_estimate=cost(64 * sites, 64 * sites),
    )(field, bonds)


def measure_kernel(side, base_ref, forward_ref, partner_ref, factors_ref, *rest):
    out_ref = rest[-1]
    coefs = [split(factors_ref[k : k + 1, :]) for k in range(4)]
    wraps = (factors_ref.shape[0] - 4) // 2
    forward, partner = split(forward_ref[...]), split(partner_ref[...])
    for wrap in range(wraps):
        scale_up = split(factors_ref[4 + wrap : 5 + wrap, :])
        scale_down = split(factors_ref[4 + wraps + wrap : 5 + wraps + wrap, :])
        forward = [u * s for u, s in zip(forward, scale_up)]
        partner = [u * s for u, s in zip(partner, scale_down)]
        hop_forward, hop_partner = hops(forward, side, coefs), hops(partner, side, coefs)
        half_forward = [u + 0.5 * h for u, h in zip(forward, hop_forward)]
        half_partner = [u - 0.5 * h for u, h in zip(partner, hop_partner)]
        hop_forward, hop_partner = hops(half_forward, side, coefs), hops(half_partner, side, coefs)
        forward = [u + h for u, h in zip(forward, hop_forward)]
        partner = [u - h for u, h in zip(partner, hop_partner)]
    row = lax.broadcasted_iota(jnp.int32, forward[0].shape, 0) + base_ref[0]
    lane = lax.broadcasted_iota(jnp.int32, forward[0].shape, 1)
    for j, (f, p) in enumerate(zip(forward, partner)):
        term = jnp.where(lane + j * LANES == row, 0.0, f * p)
        out_ref[:, j * LANES : (j + 1) * LANES] = term.astype(out_ref.dtype)


def measured(base, forward, partner, rates, *kept):
    return pl.pallas_call(
        functools.partial(measure_kernel, math.isqrt(forward.shape[1])),
        out_shape=jax.ShapeDtypeStruct(forward.shape, jnp.bfloat16),
        in_specs=[SMEM, VMEM, VMEM, VMEM] + [ANY] * len(kept),
        out_specs=VMEM,
        compiler_params=params(),
        cost_estimate=cost(200 * forward.size, 12 * forward.size),
    )(base, forward, partner, rates, *kept)


def packed_kernel(base_ref, columns_ref, rows_ref, forward_low, partner_low, forward_ref, partner_ref, rows, arrived):
    copies = [
        pltpu.make_async_copy(columns_ref, forward_ref, arrived.at[0]),
        pltpu.make_async_copy(rows_ref, rows, arrived.at[1]),
    ]
    for copy in copies:
        copy.start()
    for copy in copies:
        copy.wait()
    row = lax.broadcasted_iota(jnp.int32, rows.shape, 0) + base_ref[0]
    lane = lax.broadcasted_iota(jnp.int32, rows.shape, 1)
    partner = jnp.where(lane == row, rows[...] - 1.0, rows[...])
    partner_ref[...] = partner
    partner_low[...] = partner.astype(partner_low.dtype)
    forward_low[...] = forward_ref[...].astype(forward_low.dtype)


def packed(base, columns, rows):
    low = jax.ShapeDtypeStruct(rows.shape, jnp.bfloat16)
    full = jax.ShapeDtypeStruct(rows.shape, jnp.float32)
    return pl.pallas_call(
        packed_kernel,
        out_shape=(low, low, full, full),
        in_specs=[SMEM, ANY, ANY],
        out_specs=(VMEM,) * 4,
        scratch_shapes=[pltpu.VMEM(rows.shape, rows.dtype), pltpu.SemaphoreType.DMA((2,))],
        compiler_params=params(),
        cost_estimate=cost(4 * rows.size, 12 * rows.size),
    )(
        base,
        pltpu.with_memory_space_constraint(columns, pltpu.HBM),
        pltpu.with_memory_space_constraint(rows, pltpu.HBM),
    )


def turned_kernel(map_ref, out_ref, held, arrived):
    rows = held.shape[1]
    copies = [
        pltpu.make_async_copy(map_ref.at[pl.ds(part * rows, rows)], held.at[part], arrived.at[part])
        for part in range(held.shape[0])
    ]
    for copy in copies:
        copy.start()
    for part, copy in enumerate(copies):
        copy.wait()
        out_ref[:, part * rows : (part + 1) * rows] = held[part].T


def turned(dense):
    parts = 4
    rows, columns = dense.shape[0] // parts, dense.shape[1]
    return pl.pallas_call(
        turned_kernel,
        out_shape=jax.ShapeDtypeStruct(dense.shape[::-1], dense.dtype),
        in_specs=[ANY],
        out_specs=VMEM,
        scratch_shapes=[pltpu.VMEM((parts, rows, columns), dense.dtype), pltpu.SemaphoreType.DMA((parts,))],
        compiler_params=params(8),
        cost_estimate=cost(dense.size, 4 * dense.size),
    )(pltpu.with_memory_space_constraint(dense, pltpu.HBM))


def per_device(cluster_maps, inverse_maps, seed_columns, seed_rows, ising_field, hop_bonds):
    clusters = lax.axis_size("tm")
    anchor = lax.axis_index("tm")
    ref_rows, sites = seed_columns.shape[1:]
    cores = lax.axis_size("col")
    core = lax.axis_index("col")

    def first_ref(displacement):
        origin = (core - (displacement > anchor).astype(jnp.int32)) % cores
        return (lax.axis_index("src") * cores + origin) * ref_rows

    def route(targets):
        return [
            (k * cores + c, t * cores + (c + shift) % cores)
            for k, (t, shift) in targets.items()
            for c in range(cores)
        ]

    around = route({k: ((k + 1) % clusters, (k + 1) // clusters) for k in range(clusters)})
    forward_map, inverse_map = turned(cluster_maps[0]), inverse_maps[0]
    rates = factors(ising_field[0], hop_bonds)
    first = first_ref(0)[None]
    forward_low, partner_low, forward, partner = packed(first, seed_columns[0], seed_rows[0])
    start = (forward, partner)

    terms = []
    for displacement in range(1, clusters):
        low = jnp.concatenate([forward_low, partner_low])
        if displacement >= 3:
            low, *terms[: displacement - 1] = lax.optimization_barrier((low, *terms[: displacement - 1]))
        low = lax.ppermute(low, ("tm", "col"), around)
        forward = jnp.dot(low[:ref_rows], forward_map, preferred_element_type=jnp.float32)
        partner = jnp.dot(low[ref_rows:], inverse_map, preferred_element_type=jnp.float32)
        forward_low, partner_low = forward.astype(jnp.bfloat16), partner.astype(jnp.bfloat16)
        if displacement == 1:
            rates, *start = lax.optimization_barrier((rates, *start, forward_low))[:3]
            terms.append(measured(first, *start, rates))
        kept = (forward_map,) if displacement == clusters - 1 else ()
        terms.append(measured(first_ref(displacement)[None], forward, partner, rates, *kept))
    last = clusters - 1
    *early, late = terms
    early = jnp.stack(early)

    def early_term(target):
        return lax.dynamic_index_in_dim(early, jnp.minimum(target, last - 1), 0, keepdims=False)

    def sent(term, targets):
        return lax.ppermute(term, ("tm", "col"), route(targets))

    def shifted(step):
        return {k: ((k + step) % clusters, -(k < (k + step) % clusters)) for k in range(clusters)}

    arrived = [sent(early_term((anchor + step) % clusters), shifted(step)) for step in range(clusters - 2, 0, -1)]
    soon = sum(term.astype(jnp.float32) for term in arrived)

    total = jnp.where(anchor == last, late, early_term(anchor)).astype(jnp.float32)
    total = total + jnp.where(anchor == last, 0.0, soon)
    total = total + sent(jnp.where(anchor == 0, late, early_term(anchor - 1)), shifted(-1)).astype(jnp.float32)
    for k in range(last - 1, 0, -1):
        total = total + sent(late, {k: (last, -1)}).astype(jnp.float32)
    return (total * (sites / clusters))[None]


def solution(mesh):
    in_specs = (
        P("tm", "chain", None),
        P("tm", "chain", None),
        P("tm", ("src", "col"), "chain"),
        P("tm", ("src", "col"), "chain"),
        P("tm", "chain", None),
        P(),
    )
    out_specs = P("tm", ("src", "col"), "chain")
    return jax.shard_map(
        per_device, mesh=mesh, in_specs=in_specs, out_specs=out_specs, check_vma=False
    )
```

```python
import functools
import math

import jax
import jax.numpy as jnp
from jax import lax
from jax.experimental import pallas as pl
from jax.experimental.pallas import tpu as pltpu
from jax.sharding import PartitionSpec as P

time_step = 0.25
field_coupling = math.log(math.exp(0.5) + math.sqrt(math.exp(1.0) - 1.0))

LANES = 128
SUBLANES = 8
VMEM = pl.BlockSpec(memory_space=pltpu.VMEM)
SMEM = pl.BlockSpec(memory_space=pltpu.SMEM)
ANY = pl.BlockSpec(memory_space=pl.ANY)


def params(mebibytes=4):
    return pltpu.CompilerParams(vmem_limit_bytes=mebibytes << 20)


def cost(flops, bytes_accessed):
    return pl.CostEstimate(flops=flops, bytes_accessed=bytes_accessed, transcendentals=0)


def rolled(blocks, shift):
    return [pltpu.roll(block, shift % LANES, 1) for block in blocks]


def split(values):
    return [values[:, j : j + LANES] for j in range(0, values.shape[1], LANES)]


def leads(blocks, side):
    return rolled(blocks, -side), rolled(blocks, side)


def beside(blocks, rows, side):
    column = lax.broadcasted_iota(jnp.int32, blocks[0].shape, 1) % side
    ahead, behind = rows
    right = [jnp.where(column == 0, q, u) for q, u in zip(behind, blocks)]
    left = [jnp.where(column == side - 1, q, u) for q, u in zip(ahead, blocks)]
    return rolled(right, -1), rolled(left, 1)


def hops(rows, columns, side, coefs):
    (ahead, behind), (right, left) = rows, columns
    count = len(ahead)
    lane = lax.broadcasted_iota(jnp.int32, ahead[0].shape, 1)
    out = []
    for j in range(count):
        row_ahead = jnp.where(lane < LANES - side, ahead[j], ahead[(j + 1) % count])
        row_behind = jnp.where(lane >= side, behind[j], behind[j - 1])
        up, down, forth, back = [c[j] for c in coefs]
        out.append((up * row_ahead + down * row_behind) + (forth * right[j] + back * left[j]))
    return out


def factors_kernel(side, field_ref, bonds_ref, out_ref):
    weights = bonds_ref[...].astype(jnp.float32) * time_step
    rows, columns = split(weights[0:1]), split(weights[1:2])
    lane = lax.broadcasted_iota(jnp.int32, rows[0].shape, 1)
    moved = rolled(rows, side)
    wrapped, left = rolled(columns, 1 - side), rolled(columns, 1)
    for j in range(len(rows)):
        place = slice(j * LANES, (j + 1) * LANES)
        out_ref[0:1, place] = rows[j]
        out_ref[1:2, place] = jnp.where(lane >= side, moved[j], moved[j - 1])
        out_ref[2:3, place] = columns[j]
        out_ref[3:4, place] = jnp.where(lane % side == 0, wrapped[j], left[j])
    spins = (2 * field_ref[...] - 1).astype(jnp.float32)
    wraps = spins.shape[0]
    out_ref[4 : 4 + wraps, :] = jnp.exp(field_coupling * spins)
    out_ref[4 + wraps : 4 + 2 * wraps, :] = jnp.exp(-field_coupling * spins)


def factors(field, bonds):
    wraps, sites = field.shape
    return pl.pallas_call(
        functools.partial(factors_kernel, math.isqrt(sites)),
        out_shape=jax.ShapeDtypeStruct((4 + 2 * wraps, sites), jnp.float32),
        in_specs=[VMEM, VMEM],
        out_specs=VMEM,
        compiler_params=params(),
        cost_estimate=cost(64 * sites, 64 * sites),
    )(field, bonds)


def measure_kernel(side, base_ref, forward_ref, partner_ref, factors_ref, out_ref):
    total = forward_ref.shape[0]
    count = SUBLANES if total % SUBLANES == 0 else total
    wraps = (factors_ref.shape[0] - 4) // 2
    coefs = [split(factors_ref[k : k + 1, :]) for k in range(4)]
    halves = [[0.5 * c for c in blocks] for blocks in coefs]
    groups = range(0, total, count)
    chains = [(ref, row, sign, place) for row in groups for ref, sign, place in ((forward_ref, 1.0, 4), (partner_ref, -1.0, 4 + wraps))]
    values = [split(ref[row : row + count, :]) for ref, row, _, _ in chains]
    for wrap in range(wraps):
        scales = {place: split(factors_ref[place + wrap : place + wrap + 1, :]) for place in (4, 4 + wraps)}
        values = [[u * s for u, s in zip(v, scales[place])] for v, (_, _, _, place) in zip(values, chains)]
        inner = values
        for weights in (halves, coefs):
            rows = [leads(v, side) for v in inner]
            columns = [beside(v, r, side) for v, r in zip(inner, rows)]
            inner = [
                [u + h if sign > 0 else u - h for u, h in zip(v, hops(r, c, side, weights))]
                for v, r, c, (_, _, sign, _) in zip(values, rows, columns, chains)
            ]
        values = inner
    lane = lax.broadcasted_iota(jnp.int32, (count, LANES), 1)
    for row, forward, partner in zip(groups, values[0::2], values[1::2]):
        site = lax.broadcasted_iota(jnp.int32, (count, LANES), 0) + base_ref[0] + row
        for j, (f, p) in enumerate(zip(forward, partner)):
            term = jnp.where(lane + j * LANES == site, 0.0, f * p)
            out_ref[row : row + count, j * LANES : (j + 1) * LANES] = term.astype(out_ref.dtype)


def measured(base, forward, partner, rates):
    return pl.pallas_call(
        functools.partial(measure_kernel, math.isqrt(forward.shape[1])),
        out_shape=jax.ShapeDtypeStruct(forward.shape, jnp.bfloat16),
        in_specs=[SMEM, VMEM, VMEM, VMEM],
        out_specs=VMEM,
        compiler_params=params(),
        cost_estimate=cost(45000 * forward.size, 12 * forward.size),
    )(base, forward, partner, rates)


def packed_kernel(base_ref, columns_ref, rows_ref, forward_low, partner_low, forward_ref, partner_ref, rows, arrived):
    copies = [
        pltpu.make_async_copy(columns_ref, forward_ref, arrived.at[0]),
        pltpu.make_async_copy(rows_ref, rows, arrived.at[1]),
    ]
    for copy in copies:
        copy.start()
    for copy in copies:
        copy.wait()
    row = lax.broadcasted_iota(jnp.int32, rows.shape, 0) + base_ref[0]
    lane = lax.broadcasted_iota(jnp.int32, rows.shape, 1)
    partner = jnp.where(lane == row, rows[...] - 1.0, rows[...])
    partner_ref[...] = partner
    partner_low[...] = partner.astype(partner_low.dtype)
    forward_low[...] = forward_ref[...].astype(forward_low.dtype)


def packed(base, columns, rows):
    low = jax.ShapeDtypeStruct(rows.shape, jnp.bfloat16)
    full = jax.ShapeDtypeStruct(rows.shape, jnp.float32)
    return pl.pallas_call(
        packed_kernel,
        out_shape=(low, low, full, full),
        in_specs=[SMEM, ANY, ANY],
        out_specs=(VMEM,) * 4,
        scratch_shapes=[pltpu.VMEM(rows.shape, rows.dtype), pltpu.SemaphoreType.DMA((2,))],
        compiler_params=params(),
        cost_estimate=cost(4 * rows.size, 12 * rows.size),
    )(
        base,
        pltpu.with_memory_space_constraint(columns, pltpu.HBM),
        pltpu.with_memory_space_constraint(rows, pltpu.HBM),
    )


def turned_kernel(map_ref, out_ref, held, arrived):
    rows = held.shape[1]
    copies = [
        pltpu.make_async_copy(map_ref.at[pl.ds(part * rows, rows)], held.at[part], arrived.at[part])
        for part in range(held.shape[0])
    ]
    for copy in copies:
        copy.start()
    for part, copy in enumerate(copies):
        copy.wait()
        out_ref[:, part * rows : (part + 1) * rows] = held[part].T


def turned(dense):
    parts = 4
    rows, columns = dense.shape[0] // parts, dense.shape[1]
    return pl.pallas_call(
        turned_kernel,
        out_shape=jax.ShapeDtypeStruct(dense.shape[::-1], dense.dtype),
        in_specs=[ANY],
        out_specs=VMEM,
        scratch_shapes=[pltpu.VMEM((parts, rows, columns), dense.dtype), pltpu.SemaphoreType.DMA((parts,))],
        compiler_params=params(8),
        cost_estimate=cost(dense.size, 4 * dense.size),
    )(pltpu.with_memory_space_constraint(dense, pltpu.HBM))


def per_device(cluster_maps, inverse_maps, seed_columns, seed_rows, ising_field, hop_bonds):
    clusters = lax.axis_size("tm")
    anchor = lax.axis_index("tm")
    ref_rows, sites = seed_columns.shape[1:]
    cores = lax.axis_size("col")
    core = lax.axis_index("col")

    def first_ref(displacement):
        origin = (core - (displacement > anchor).astype(jnp.int32)) % cores
        return (lax.axis_index("src") * cores + origin) * ref_rows

    def route(targets):
        return [
            (k * cores + c, t * cores + (c + shift) % cores)
            for k, (t, shift) in targets.items()
            for c in range(cores)
        ]

    around = route({k: ((k + 1) % clusters, (k + 1) // clusters) for k in range(clusters)})
    forward_map, inverse_map = turned(cluster_maps[0]), inverse_maps[0]
    rates = factors(ising_field[0], hop_bonds)
    first = first_ref(0)[None]
    forward_low, partner_low, forward, partner = packed(first, seed_columns[0], seed_rows[0])
    start = (forward, partner)

    terms = []
    for displacement in range(1, clusters):
        low = jnp.concatenate([forward_low, partner_low])
        if displacement >= 3:
            low, *terms[: displacement - 1] = lax.optimization_barrier((low, *terms[: displacement - 1]))
        low = lax.ppermute(low, ("tm", "col"), around)
        forward = jnp.dot(low[:ref_rows], forward_map, preferred_element_type=jnp.float32)
        partner = jnp.dot(low[ref_rows:], inverse_map, preferred_element_type=jnp.float32)
        forward_low, partner_low = forward.astype(jnp.bfloat16), partner.astype(jnp.bfloat16)
        if displacement == 1:
            rates, *start = lax.optimization_barrier((rates, *start, forward_low))[:3]
            terms.append(measured(first, *start, rates))
        terms.append(measured(first_ref(displacement)[None], forward, partner, rates))
    last = clusters - 1
    *early, late = terms
    early = jnp.stack(early)

    def early_term(target):
        return lax.dynamic_index_in_dim(early, jnp.minimum(target, last - 1), 0, keepdims=False)

    def sent(term, targets):
        return lax.ppermute(term, ("tm", "col"), route(targets))

    def shifted(step):
        return {k: ((k + step) % clusters, -(k < (k + step) % clusters)) for k in range(clusters)}

    arrived = [sent(early_term((anchor + step) % clusters), shifted(step)) for step in range(clusters - 2, 0, -1)]
    soon = sum(term.astype(jnp.float32) for term in arrived)

    total = jnp.where(anchor == last, late, early_term(anchor)).astype(jnp.float32)
    total = total + jnp.where(anchor == last, 0.0, soon)
    others = [sent(late, {k: (last, -1)}) for k in range(1, last - 1)]
    beside = sent(late, {k: (k ^ 1, -(k < k ^ 1)) for k in range(clusters)})
    behind = sent(jnp.where(anchor == 0, late, early_term(anchor - 1)), shifted(-1))
    total = total + sum(term.astype(jnp.float32) for term in others)
    total = total + jnp.where(anchor == last, beside, 0.0).astype(jnp.float32)
    total = total + behind.astype(jnp.float32)
    return (total * (sites / clusters))[None]


def solution(mesh):
    in_specs = (
        P("tm", "chain", None),
        P("tm", "chain", None),
        P("tm", ("src", "col"), "chain"),
        P("tm", ("src", "col"), "chain"),
        P("tm", "chain", None),
        P(),
    )
    out_specs = P("tm", ("src", "col"), "chain")
    return jax.shard_map(
        per_device, mesh=mesh, in_specs=in_specs, out_specs=out_specs, check_vma=False
    )
```

```python
import functools
import math

import jax
import jax.numpy as jnp
from jax import lax
from jax.experimental import pallas as pl
from jax.experimental.pallas import tpu as pltpu
from jax.sharding import PartitionSpec as P

time_step = 0.25
field_coupling = math.log(math.exp(0.5) + math.sqrt(math.exp(1.0) - 1.0))

LANES = 128
SUBLANES = 8
VMEM = pl.BlockSpec(memory_space=pltpu.VMEM)
SMEM = pl.BlockSpec(memory_space=pltpu.SMEM)
ANY = pl.BlockSpec(memory_space=pl.ANY)


def params(mebibytes=4):
    return pltpu.CompilerParams(vmem_limit_bytes=mebibytes << 20)


def cost(flops, bytes_accessed):
    return pl.CostEstimate(flops=flops, bytes_accessed=bytes_accessed, transcendentals=0)


def rolled(blocks, shift):
    return [pltpu.roll(block, shift % LANES, 1) for block in blocks]


def split(values):
    return [values[:, j : j + LANES] for j in range(0, values.shape[1], LANES)]


def leads(blocks, side):
    return rolled(blocks, -side), rolled(blocks, side)


def beside(blocks, rows, side):
    column = lax.broadcasted_iota(jnp.int32, blocks[0].shape, 1) % side
    ahead, behind = rows
    right = [jnp.where(column == 0, q, u) for q, u in zip(behind, blocks)]
    left = [jnp.where(column == side - 1, q, u) for q, u in zip(ahead, blocks)]
    return rolled(right, -1), rolled(left, 1)


def hops(rows, columns, side, coefs):
    (ahead, behind), (right, left) = rows, columns
    count = len(ahead)
    lane = lax.broadcasted_iota(jnp.int32, ahead[0].shape, 1)
    out = []
    for j in range(count):
        row_ahead = jnp.where(lane < LANES - side, ahead[j], ahead[(j + 1) % count])
        row_behind = jnp.where(lane >= side, behind[j], behind[j - 1])
        up, down, forth, back = [c[j] for c in coefs]
        out.append((up * row_ahead + down * row_behind) + (forth * right[j] + back * left[j]))
    return out


def factors_kernel(side, field_ref, bonds_ref, out_ref):
    weights = bonds_ref[...].astype(jnp.float32) * time_step
    rows, columns = split(weights[0:1]), split(weights[1:2])
    lane = lax.broadcasted_iota(jnp.int32, rows[0].shape, 1)
    moved = rolled(rows, side)
    wrapped, left = rolled(columns, 1 - side), rolled(columns, 1)
    for j in range(len(rows)):
        place = slice(j * LANES, (j + 1) * LANES)
        out_ref[0:1, place] = rows[j]
        out_ref[1:2, place] = jnp.where(lane >= side, moved[j], moved[j - 1])
        out_ref[2:3, place] = columns[j]
        out_ref[3:4, place] = jnp.where(lane % side == 0, wrapped[j], left[j])
    spins = (2 * field_ref[...] - 1).astype(jnp.float32)
    wraps = spins.shape[0]
    out_ref[4 : 4 + wraps, :] = jnp.exp(field_coupling * spins)
    out_ref[4 + wraps : 4 + 2 * wraps, :] = jnp.exp(-field_coupling * spins)


def factors(field, bonds):
    wraps, sites = field.shape
    return pl.pallas_call(
        functools.partial(factors_kernel, math.isqrt(sites)),
        out_shape=jax.ShapeDtypeStruct((4 + 2 * wraps, sites), jnp.float32),
        in_specs=[VMEM, VMEM],
        out_specs=VMEM,
        compiler_params=params(),
        cost_estimate=cost(64 * sites, 64 * sites),
    )(field, bonds)


def measure_kernel(side, base_ref, forward_ref, partner_ref, factors_ref, out_ref):
    total = forward_ref.shape[0]
    count = SUBLANES if total % SUBLANES == 0 else total
    wraps = (factors_ref.shape[0] - 4) // 2
    coefs = [split(factors_ref[k : k + 1, :]) for k in range(4)]
    halves = [[0.5 * c for c in blocks] for blocks in coefs]
    groups = range(0, total, count)
    chains = [(ref, row, sign, place) for row in groups for ref, sign, place in ((forward_ref, 1.0, 4), (partner_ref, -1.0, 4 + wraps))]
    values = [split(ref[row : row + count, :]) for ref, row, _, _ in chains]
    for wrap in range(wraps):
        scales = {place: split(factors_ref[place + wrap : place + wrap + 1, :]) for place in (4, 4 + wraps)}
        values = [[u * s for u, s in zip(v, scales[place])] for v, (_, _, _, place) in zip(values, chains)]
        inner = values
        for weights in (halves, coefs):
            rows = [leads(v, side) for v in inner]
            columns = [beside(v, r, side) for v, r in zip(inner, rows)]
            inner = [
                [u + h if sign > 0 else u - h for u, h in zip(v, hops(r, c, side, weights))]
                for v, r, c, (_, _, sign, _) in zip(values, rows, columns, chains)
            ]
        values = inner
    lane = lax.broadcasted_iota(jnp.int32, (count, LANES), 1)
    for row, forward, partner in zip(groups, values[0::2], values[1::2]):
        site = lax.broadcasted_iota(jnp.int32, (count, LANES), 0) + base_ref[0] + row
        for j, (f, p) in enumerate(zip(forward, partner)):
            term = jnp.where(lane + j * LANES == site, 0.0, f * p)
            out_ref[row : row + count, j * LANES : (j + 1) * LANES] = term.astype(out_ref.dtype)


def measured(base, forward, partner, rates):
    return pl.pallas_call(
        functools.partial(measure_kernel, math.isqrt(forward.shape[1])),
        out_shape=jax.ShapeDtypeStruct(forward.shape, jnp.bfloat16),
        in_specs=[SMEM, VMEM, VMEM, VMEM],
        out_specs=VMEM,
        compiler_params=params(),
        cost_estimate=cost(45000 * forward.size, 12 * forward.size),
    )(base, forward, partner, rates)


def packed_kernel(base_ref, columns_ref, rows_ref, forward_low, partner_low, forward_ref, partner_ref, rows, arrived):
    copies = [
        pltpu.make_async_copy(columns_ref, forward_ref, arrived.at[0]),
        pltpu.make_async_copy(rows_ref, rows, arrived.at[1]),
    ]
    for copy in copies:
        copy.start()
    for copy in copies:
        copy.wait()
    row = lax.broadcasted_iota(jnp.int32, rows.shape, 0) + base_ref[0]
    lane = lax.broadcasted_iota(jnp.int32, rows.shape, 1)
    partner = jnp.where(lane == row, rows[...] - 1.0, rows[...])
    partner_ref[...] = partner
    partner_low[...] = partner.astype(partner_low.dtype)
    forward_low[...] = forward_ref[...].astype(forward_low.dtype)


def packed(base, columns, rows):
    low = jax.ShapeDtypeStruct(rows.shape, jnp.bfloat16)
    full = jax.ShapeDtypeStruct(rows.shape, jnp.float32)
    return pl.pallas_call(
        packed_kernel,
        out_shape=(low, low, full, full),
        in_specs=[SMEM, ANY, ANY],
        out_specs=(VMEM,) * 4,
        scratch_shapes=[pltpu.VMEM(rows.shape, rows.dtype), pltpu.SemaphoreType.DMA((2,))],
        compiler_params=params(),
        cost_estimate=cost(4 * rows.size, 12 * rows.size),
    )(
        base,
        pltpu.with_memory_space_constraint(columns, pltpu.HBM),
        pltpu.with_memory_space_constraint(rows, pltpu.HBM),
    )


def turned_kernel(map_ref, out_ref, held, arrived):
    rows = held.shape[1]
    copies = [
        pltpu.make_async_copy(map_ref.at[pl.ds(part * rows, rows)], held.at[part], arrived.at[part])
        for part in range(held.shape[0])
    ]
    for copy in copies:
        copy.start()
    for part, copy in enumerate(copies):
        copy.wait()
        out_ref[:, part * rows : (part + 1) * rows] = held[part].T


def turned(dense):
    parts = 4
    rows, columns = dense.shape[0] // parts, dense.shape[1]
    return pl.pallas_call(
        turned_kernel,
        out_shape=jax.ShapeDtypeStruct(dense.shape[::-1], dense.dtype),
        in_specs=[ANY],
        out_specs=VMEM,
        scratch_shapes=[pltpu.VMEM((parts, rows, columns), dense.dtype), pltpu.SemaphoreType.DMA((parts,))],
        compiler_params=params(8),
        cost_estimate=cost(dense.size, 4 * dense.size),
    )(pltpu.with_memory_space_constraint(dense, pltpu.HBM))


def per_device(cluster_maps, inverse_maps, seed_columns, seed_rows, ising_field, hop_bonds):
    clusters = lax.axis_size("tm")
    anchor = lax.axis_index("tm")
    ref_rows, sites = seed_columns.shape[1:]
    cores = lax.axis_size("col")
    core = lax.axis_index("col")

    def first_ref(displacement):
        origin = (core - (displacement > anchor).astype(jnp.int32)) % cores
        return (lax.axis_index("src") * cores + origin) * ref_rows

    def route(targets):
        return [
            (k * cores + c, t * cores + (c + shift) % cores)
            for k, (t, shift) in targets.items()
            for c in range(cores)
        ]

    around = route({k: ((k + 1) % clusters, (k + 1) // clusters) for k in range(clusters)})
    forward_map, inverse_map = turned(cluster_maps[0]), inverse_maps[0]
    first = first_ref(0)[None]
    forward_low, partner_low, forward, partner = packed(first, seed_columns[0], seed_rows[0])
    start = (forward, partner)

    terms = []
    for displacement in range(1, clusters):
        low = jnp.concatenate([forward_low, partner_low])
        if displacement >= 3:
            low, *terms[: displacement - 1] = lax.optimization_barrier((low, *terms[: displacement - 1]))
        low = lax.ppermute(low, ("tm", "col"), around)
        forward = jnp.dot(low[:ref_rows], forward_map, preferred_element_type=jnp.float32)
        partner = jnp.dot(low[ref_rows:], inverse_map, preferred_element_type=jnp.float32)
        forward_low, partner_low = forward.astype(jnp.bfloat16), partner.astype(jnp.bfloat16)
        if displacement == 1:
            field, bonds, *start = lax.optimization_barrier((ising_field[0], hop_bonds, *start, forward_low))[:4]
            rates = factors(field, bonds)
            terms.append(measured(first, *start, rates))
        terms.append(measured(first_ref(displacement)[None], forward, partner, rates))
    last = clusters - 1
    *early, late = terms
    early = jnp.stack(early)

    def early_term(target):
        return lax.dynamic_index_in_dim(early, jnp.minimum(target, last - 1), 0, keepdims=False)

    def sent(term, targets):
        return lax.ppermute(term, ("tm", "col"), route(targets))

    def shifted(step):
        return {k: ((k + step) % clusters, -(k < (k + step) % clusters)) for k in range(clusters)}

    arrived = [sent(early_term((anchor + step) % clusters), shifted(step)) for step in range(clusters - 2, 0, -1)]
    soon = sum(term.astype(jnp.float32) for term in arrived)

    total = jnp.where(anchor == last, late, early_term(anchor)).astype(jnp.float32)
    total = total + jnp.where(anchor == last, 0.0, soon)
    behind = jnp.where(anchor == 0, late, early_term(anchor - 1))
    soonest = jnp.where(anchor == 1, late, early_term(anchor))
    soonest, behind, late = lax.optimization_barrier((soonest, behind, late))

    def sent_last(term, k):
        swap = {m: (m, 1) for m in range(clusters)}
        term = sent(term, {**swap, k: (last, -1), last: (k, 1)})
        return jnp.where(anchor == last, term, 0.0).astype(jnp.float32)

    total = total + sent_last(soonest, 1)
    for k in range(last - 1, 1, -1):
        total = total + sent_last(late, k)
    total = total + sent(behind, shifted(-1)).astype(jnp.float32)
    return (total * (sites / clusters))[None]


def solution(mesh):
    in_specs = (
        P("tm", "chain", None),
        P("tm", "chain", None),
        P("tm", ("src", "col"), "chain"),
        P("tm", ("src", "col"), "chain"),
        P("tm", "chain", None),
        P(),
    )
    out_specs = P("tm", ("src", "col"), "chain")
    return jax.shard_map(
        per_device, mesh=mesh, in_specs=in_specs, out_specs=out_specs, check_vma=False
    )
```

```python
import functools
import math

import jax
import jax.numpy as jnp
from jax import lax
from jax.experimental import pallas as pl
from jax.experimental.pallas import tpu as pltpu
from jax.sharding import PartitionSpec as P

time_step = 0.25
field_coupling = math.log(math.exp(0.5) + math.sqrt(math.exp(1.0) - 1.0))

LANES = 128
SUBLANES = 8
VMEM = pl.BlockSpec(memory_space=pltpu.VMEM)
SMEM = pl.BlockSpec(memory_space=pltpu.SMEM)
ANY = pl.BlockSpec(memory_space=pl.ANY)


def params(mebibytes=4):
    return pltpu.CompilerParams(vmem_limit_bytes=mebibytes << 20)


def cost(flops, bytes_accessed):
    return pl.CostEstimate(flops=flops, bytes_accessed=bytes_accessed, transcendentals=0)


def rolled(blocks, shift):
    return [pltpu.roll(block, shift % LANES, 1) for block in blocks]


def split(values):
    return [values[:, j : j + LANES] for j in range(0, values.shape[1], LANES)]


def leads(blocks, side):
    return rolled(blocks, -side), rolled(blocks, side)


def beside(blocks, rows, side):
    column = lax.broadcasted_iota(jnp.int32, blocks[0].shape, 1) % side
    ahead, behind = rows
    right = [jnp.where(column == 0, q, u) for q, u in zip(behind, blocks)]
    left = [jnp.where(column == side - 1, q, u) for q, u in zip(ahead, blocks)]
    return rolled(right, -1), rolled(left, 1)


def hops(rows, columns, side, coefs):
    (ahead, behind), (right, left) = rows, columns
    count = len(ahead)
    lane = lax.broadcasted_iota(jnp.int32, ahead[0].shape, 1)
    out = []
    for j in range(count):
        row_ahead = jnp.where(lane < LANES - side, ahead[j], ahead[(j + 1) % count])
        row_behind = jnp.where(lane >= side, behind[j], behind[j - 1])
        up, down, forth, back = [c[j] for c in coefs]
        out.append((up * row_ahead + down * row_behind) + (forth * right[j] + back * left[j]))
    return out


def factors_kernel(side, field_ref, bonds_ref, out_ref):
    weights = bonds_ref[...].astype(jnp.float32) * time_step
    rows, columns = split(weights[0:1]), split(weights[1:2])
    lane = lax.broadcasted_iota(jnp.int32, rows[0].shape, 1)
    moved = rolled(rows, side)
    wrapped, left = rolled(columns, 1 - side), rolled(columns, 1)
    for j in range(len(rows)):
        place = slice(j * LANES, (j + 1) * LANES)
        out_ref[0:1, place] = rows[j]
        out_ref[1:2, place] = jnp.where(lane >= side, moved[j], moved[j - 1])
        out_ref[2:3, place] = columns[j]
        out_ref[3:4, place] = jnp.where(lane % side == 0, wrapped[j], left[j])
    spins = (2 * field_ref[...] - 1).astype(jnp.float32)
    wraps = spins.shape[0]
    out_ref[4 : 4 + wraps, :] = jnp.exp(field_coupling * spins)
    out_ref[4 + wraps : 4 + 2 * wraps, :] = jnp.exp(-field_coupling * spins)


def factors(field, bonds):
    wraps, sites = field.shape
    return pl.pallas_call(
        functools.partial(factors_kernel, math.isqrt(sites)),
        out_shape=jax.ShapeDtypeStruct((4 + 2 * wraps, sites), jnp.float32),
        in_specs=[VMEM, VMEM],
        out_specs=VMEM,
        compiler_params=params(),
        cost_estimate=cost(64 * sites, 64 * sites),
    )(field, bonds)


def measure_kernel(side, base_ref, forward_ref, partner_ref, factors_ref, out_ref):
    total = forward_ref.shape[0]
    count = SUBLANES if total % SUBLANES == 0 else total
    wraps = (factors_ref.shape[0] - 4) // 2
    coefs = [split(factors_ref[k : k + 1, :]) for k in range(4)]
    halves = [[0.5 * c for c in blocks] for blocks in coefs]
    groups = range(0, total, count)
    chains = [(ref, row, sign, place) for row in groups for ref, sign, place in ((forward_ref, 1.0, 4), (partner_ref, -1.0, 4 + wraps))]
    values = [split(ref[row : row + count, :]) for ref, row, _, _ in chains]
    for wrap in range(wraps):
        scales = {place: split(factors_ref[place + wrap : place + wrap + 1, :]) for place in (4, 4 + wraps)}
        values = [[u * s for u, s in zip(v, scales[place])] for v, (_, _, _, place) in zip(values, chains)]
        inner = values
        for weights in (halves, coefs):
            rows = [leads(v, side) for v in inner]
            columns = [beside(v, r, side) for v, r in zip(inner, rows)]
            inner = [
                [u + h if sign > 0 else u - h for u, h in zip(v, hops(r, c, side, weights))]
                for v, r, c, (_, _, sign, _) in zip(values, rows, columns, chains)
            ]
        values = inner
    row = lax.broadcasted_iota(jnp.int32, (total, LANES), 0) + base_ref[0]
    lane = lax.broadcasted_iota(jnp.int32, (total, LANES), 1)
    for j in range(len(coefs[0])):
        products = [f[j] * p[j] for f, p in zip(values[0::2], values[1::2])]
        term = jnp.where(lane + j * LANES == row, 0.0, jnp.concatenate(products))
        out_ref[:, j * LANES : (j + 1) * LANES] = term.astype(out_ref.dtype)


def measured(base, forward, partner, rates):
    return pl.pallas_call(
        functools.partial(measure_kernel, math.isqrt(forward.shape[1])),
        out_shape=jax.ShapeDtypeStruct(forward.shape, jnp.bfloat16),
        in_specs=[SMEM, VMEM, VMEM, VMEM],
        out_specs=VMEM,
        compiler_params=params(),
        cost_estimate=cost(45000 * forward.size, 12 * forward.size),
    )(base, forward, partner, rates)


def packed_kernel(base_ref, columns_ref, rows_ref, forward_low, partner_low, forward_ref, partner_ref, rows, arrived):
    copies = [
        pltpu.make_async_copy(columns_ref, forward_ref, arrived.at[0]),
        pltpu.make_async_copy(rows_ref, rows, arrived.at[1]),
    ]
    for copy in copies:
        copy.start()
    for copy in copies:
        copy.wait()
    row = lax.broadcasted_iota(jnp.int32, rows.shape, 0) + base_ref[0]
    lane = lax.broadcasted_iota(jnp.int32, rows.shape, 1)
    partner = jnp.where(lane == row, rows[...] - 1.0, rows[...])
    partner_ref[...] = partner
    partner_low[...] = partner.astype(partner_low.dtype)
    forward_low[...] = forward_ref[...].astype(forward_low.dtype)


def packed(base, columns, rows):
    low = jax.ShapeDtypeStruct(rows.shape, jnp.bfloat16)
    full = jax.ShapeDtypeStruct(rows.shape, jnp.float32)
    return pl.pallas_call(
        packed_kernel,
        out_shape=(low, low, full, full),
        in_specs=[SMEM, ANY, ANY],
        out_specs=(VMEM,) * 4,
        scratch_shapes=[pltpu.VMEM(rows.shape, rows.dtype), pltpu.SemaphoreType.DMA((2,))],
        compiler_params=params(),
        cost_estimate=cost(4 * rows.size, 12 * rows.size),
    )(
        base,
        pltpu.with_memory_space_constraint(columns, pltpu.HBM),
        pltpu.with_memory_space_constraint(rows, pltpu.HBM),
    )


def turned_kernel(map_ref, out_ref, held, arrived):
    rows = held.shape[1]
    copies = [
        pltpu.make_async_copy(map_ref.at[pl.ds(part * rows, rows)], held.at[part], arrived.at[part])
        for part in range(held.shape[0])
    ]
    for copy in copies:
        copy.start()
    for part, copy in enumerate(copies):
        copy.wait()
        out_ref[:, part * rows : (part + 1) * rows] = held[part].T


def turned(dense):
    parts = 4
    rows, columns = dense.shape[0] // parts, dense.shape[1]
    return pl.pallas_call(
        turned_kernel,
        out_shape=jax.ShapeDtypeStruct(dense.shape[::-1], dense.dtype),
        in_specs=[ANY],
        out_specs=VMEM,
        scratch_shapes=[pltpu.VMEM((parts, rows, columns), dense.dtype), pltpu.SemaphoreType.DMA((parts,))],
        compiler_params=params(8),
        cost_estimate=cost(dense.size, 4 * dense.size),
    )(pltpu.with_memory_space_constraint(dense, pltpu.HBM))


def per_device(cluster_maps, inverse_maps, seed_columns, seed_rows, ising_field, hop_bonds):
    clusters = lax.axis_size("tm")
    anchor = lax.axis_index("tm")
    ref_rows, sites = seed_columns.shape[1:]
    cores = lax.axis_size("col")
    core = lax.axis_index("col")

    def first_ref(displacement):
        origin = (core - (displacement > anchor).astype(jnp.int32)) % cores
        return (lax.axis_index("src") * cores + origin) * ref_rows

    def route(targets):
        return [
            (k * cores + c, t * cores + (c + shift) % cores)
            for k, (t, shift) in targets.items()
            for c in range(cores)
        ]

    around = route({k: ((k + 1) % clusters, (k + 1) // clusters) for k in range(clusters)})
    forward_map, inverse_map = turned(cluster_maps[0]), inverse_maps[0]
    first = first_ref(0)[None]
    forward_low, partner_low, forward, partner = packed(first, seed_columns[0], seed_rows[0])
    start = (forward, partner)

    terms = []
    for displacement in range(1, clusters):
        low = jnp.concatenate([forward_low, partner_low])
        if displacement >= 3:
            low, *terms[: displacement - 1] = lax.optimization_barrier((low, *terms[: displacement - 1]))
        low = lax.ppermute(low, ("tm", "col"), around)
        forward = jnp.dot(low[:ref_rows], forward_map, preferred_element_type=jnp.float32)
        partner = jnp.dot(low[ref_rows:], inverse_map, preferred_element_type=jnp.float32)
        forward_low, partner_low = forward.astype(jnp.bfloat16), partner.astype(jnp.bfloat16)
        if displacement == 1:
            field, bonds, *start = lax.optimization_barrier((ising_field[0], hop_bonds, *start, forward_low))[:4]
            rates = factors(field, bonds)
            terms.append(measured(first, *start, rates))
        terms.append(measured(first_ref(displacement)[None], forward, partner, rates))
    last = clusters - 1
    *early, late = terms
    early = jnp.stack(early)

    def early_term(target):
        return lax.dynamic_index_in_dim(early, jnp.minimum(target, last - 1), 0, keepdims=False)

    def sent(term, targets):
        return lax.ppermute(term, ("tm", "col"), route(targets))

    def shifted(step):
        return {k: ((k + step) % clusters, -(k < (k + step) % clusters)) for k in range(clusters)}

    arrived = [sent(early_term((anchor + step) % clusters), shifted(step)) for step in range(clusters - 2, 0, -1)]
    soon = sum(term.astype(jnp.float32) for term in arrived)

    total = jnp.where(anchor == last, late, early_term(anchor)).astype(jnp.float32)
    total = total + jnp.where(anchor == last, 0.0, soon)
    behind = jnp.where(anchor == 0, late, early_term(anchor - 1))
    soonest = jnp.where(anchor == 1, late, early_term(anchor))
    soonest, behind, late = lax.optimization_barrier((soonest, behind, late))

    def sent_last(term, k):
        swap = {m: (m, 1) for m in range(clusters)}
        term = sent(term, {**swap, k: (last, -1), last: (k, 1)})
        return jnp.where(anchor == last, term, 0.0).astype(jnp.float32)

    total = total + sent_last(soonest, 1)
    for k in range(last - 1, 1, -1):
        total = total + sent_last(late, k)
    total = total + sent(behind, shifted(-1)).astype(jnp.float32)
    return (total * (sites / clusters))[None]


def solution(mesh):
    in_specs = (
        P("tm", "chain", None),
        P("tm", "chain", None),
        P("tm", ("src", "col"), "chain"),
        P("tm", ("src", "col"), "chain"),
        P("tm", "chain", None),
        P(),
    )
    out_specs = P("tm", ("src", "col"), "chain")
    return jax.shard_map(
        per_device, mesh=mesh, in_specs=in_specs, out_specs=out_specs, check_vma=False
    )
```

```python
import functools
import math

import jax
import jax.numpy as jnp
from jax import lax
from jax.experimental import pallas as pl
from jax.experimental.pallas import tpu as pltpu
from jax.sharding import PartitionSpec as P

time_step = 0.25
field_coupling = math.log(math.exp(0.5) + math.sqrt(math.exp(1.0) - 1.0))

LANES = 128
SUBLANES = 8
VMEM = pl.BlockSpec(memory_space=pltpu.VMEM)
SMEM = pl.BlockSpec(memory_space=pltpu.SMEM)
ANY = pl.BlockSpec(memory_space=pl.ANY)


def params(mebibytes=4):
    return pltpu.CompilerParams(vmem_limit_bytes=mebibytes << 20)


def cost(flops, bytes_accessed):
    return pl.CostEstimate(flops=flops, bytes_accessed=bytes_accessed, transcendentals=0)


def rolled(blocks, shift):
    return [pltpu.roll(block, shift % LANES, 1) for block in blocks]


def split(values):
    return [values[:, j : j + LANES] for j in range(0, values.shape[1], LANES)]


def leads(blocks, side):
    return rolled(blocks, -side), rolled(blocks, side)


def beside(blocks, rows, side):
    column = lax.broadcasted_iota(jnp.int32, blocks[0].shape, 1) % side
    ahead, behind = rows
    right = [jnp.where(column == 0, q, u) for q, u in zip(behind, blocks)]
    left = [jnp.where(column == side - 1, q, u) for q, u in zip(ahead, blocks)]
    return rolled(right, -1), rolled(left, 1)


def hops(rows, columns, side, coefs):
    (ahead, behind), (right, left) = rows, columns
    count = len(ahead)
    lane = lax.broadcasted_iota(jnp.int32, ahead[0].shape, 1)
    out = []
    for j in range(count):
        row_ahead = jnp.where(lane < LANES - side, ahead[j], ahead[(j + 1) % count])
        row_behind = jnp.where(lane >= side, behind[j], behind[j - 1])
        up, down, forth, back = [c[j] for c in coefs]
        out.append((up * row_ahead + down * row_behind) + (forth * right[j] + back * left[j]))
    return out


def factors_kernel(side, field_ref, bonds_ref, out_ref):
    weights = bonds_ref[...].astype(jnp.float32) * time_step
    rows, columns = split(weights[0:1]), split(weights[1:2])
    lane = lax.broadcasted_iota(jnp.int32, rows[0].shape, 1)
    moved = rolled(rows, side)
    wrapped, left = rolled(columns, 1 - side), rolled(columns, 1)
    for j in range(len(rows)):
        place = slice(j * LANES, (j + 1) * LANES)
        out_ref[0:1, place] = rows[j]
        out_ref[1:2, place] = jnp.where(lane >= side, moved[j], moved[j - 1])
        out_ref[2:3, place] = columns[j]
        out_ref[3:4, place] = jnp.where(lane % side == 0, wrapped[j], left[j])
    spins = (2 * field_ref[...] - 1).astype(jnp.float32)
    wraps = spins.shape[0]
    out_ref[4 : 4 + wraps, :] = jnp.exp(field_coupling * spins)
    out_ref[4 + wraps : 4 + 2 * wraps, :] = jnp.exp(-field_coupling * spins)


def factors(field, bonds):
    wraps, sites = field.shape
    return pl.pallas_call(
        functools.partial(factors_kernel, math.isqrt(sites)),
        out_shape=jax.ShapeDtypeStruct((4 + 2 * wraps, sites), jnp.float32),
        in_specs=[VMEM, VMEM],
        out_specs=VMEM,
        compiler_params=params(),
        cost_estimate=cost(64 * sites, 64 * sites),
    )(field, bonds)


def measure_kernel(side, base_ref, forward_ref, partner_ref, factors_ref, out_ref):
    total = forward_ref.shape[0]
    count = SUBLANES if total % SUBLANES == 0 else total
    wraps = (factors_ref.shape[0] - 4) // 2
    coefs = [split(factors_ref[k : k + 1, :]) for k in range(4)]
    halves = [[0.5 * c for c in blocks] for blocks in coefs]
    groups = range(0, total, count)
    chains = [(ref, row, sign, place) for row in groups for ref, sign, place in ((forward_ref, 1.0, 4), (partner_ref, -1.0, 4 + wraps))]
    values = [split(ref[row : row + count, :]) for ref, row, _, _ in chains]
    for wrap in range(wraps):
        scales = {place: split(factors_ref[place + wrap : place + wrap + 1, :]) for place in (4, 4 + wraps)}
        values = [[u * s for u, s in zip(v, scales[place])] for v, (_, _, _, place) in zip(values, chains)]
        inner = values
        for weights in (halves, coefs):
            rows = [leads(v, side) for v in inner]
            columns = [beside(v, r, side) for v, r in zip(inner, rows)]
            inner = [
                [u + h if sign > 0 else u - h for u, h in zip(v, hops(r, c, side, weights))]
                for v, r, c, (_, _, sign, _) in zip(values, rows, columns, chains)
            ]
        values = inner
    row = lax.broadcasted_iota(jnp.int32, (total, LANES), 0) + base_ref[0]
    lane = lax.broadcasted_iota(jnp.int32, (total, LANES), 1)
    for j in range(len(coefs[0])):
        products = [f[j] * p[j] for f, p in zip(values[0::2], values[1::2])]
        term = jnp.where(lane + j * LANES == row, 0.0, jnp.concatenate(products))
        out_ref[:, j * LANES : (j + 1) * LANES] = term.astype(out_ref.dtype)


def measured(base, forward, partner, rates):
    return pl.pallas_call(
        functools.partial(measure_kernel, math.isqrt(forward.shape[1])),
        out_shape=jax.ShapeDtypeStruct(forward.shape, jnp.bfloat16),
        in_specs=[SMEM, VMEM, VMEM, VMEM],
        out_specs=VMEM,
        compiler_params=params(),
        cost_estimate=cost(45000 * forward.size, 12 * forward.size),
    )(base, forward, partner, rates)


def packed_kernel(base_ref, columns_ref, rows_ref, forward_low, partner_low, forward_ref, partner_ref, rows, arrived):
    copies = [
        pltpu.make_async_copy(columns_ref, forward_ref, arrived.at[0]),
        pltpu.make_async_copy(rows_ref, rows, arrived.at[1]),
    ]
    for copy in copies:
        copy.start()
    copies[0].wait()
    forward_low[...] = forward_ref[...].astype(forward_low.dtype)
    copies[1].wait()
    row = lax.broadcasted_iota(jnp.int32, rows.shape, 0) + base_ref[0]
    lane = lax.broadcasted_iota(jnp.int32, rows.shape, 1)
    partner = jnp.where(lane == row, rows[...] - 1.0, rows[...])
    partner_ref[...] = partner
    partner_low[...] = partner.astype(partner_low.dtype)


def packed(base, columns, rows):
    low = jax.ShapeDtypeStruct(rows.shape, jnp.bfloat16)
    full = jax.ShapeDtypeStruct(rows.shape, jnp.float32)
    return pl.pallas_call(
        packed_kernel,
        out_shape=(low, low, full, full),
        in_specs=[SMEM, ANY, ANY],
        out_specs=(VMEM,) * 4,
        scratch_shapes=[pltpu.VMEM(rows.shape, rows.dtype), pltpu.SemaphoreType.DMA((2,))],
        compiler_params=params(),
        cost_estimate=cost(4 * rows.size, 12 * rows.size),
    )(
        base,
        pltpu.with_memory_space_constraint(columns, pltpu.HBM),
        pltpu.with_memory_space_constraint(rows, pltpu.HBM),
    )


def turned_kernel(map_ref, out_ref, held, arrived):
    rows = held.shape[1]
    copies = [
        pltpu.make_async_copy(map_ref.at[pl.ds(part * rows, rows)], held.at[part], arrived.at[part])
        for part in range(held.shape[0])
    ]
    for copy in copies:
        copy.start()
    for part, copy in enumerate(copies):
        copy.wait()
        out_ref[:, part * rows : (part + 1) * rows] = held[part].T


def turned(dense):
    parts = 4
    rows, columns = dense.shape[0] // parts, dense.shape[1]
    return pl.pallas_call(
        turned_kernel,
        out_shape=jax.ShapeDtypeStruct(dense.shape[::-1], dense.dtype),
        in_specs=[ANY],
        out_specs=VMEM,
        scratch_shapes=[pltpu.VMEM((parts, rows, columns), dense.dtype), pltpu.SemaphoreType.DMA((parts,))],
        compiler_params=params(8),
        cost_estimate=cost(dense.size, 4 * dense.size),
    )(pltpu.with_memory_space_constraint(dense, pltpu.HBM))


def finished_kernel(scale, known_ref, arrived_ref, out_ref, held, sent):
    held[...] = (known_ref[...] + arrived_ref[...].astype(jnp.float32)) * scale
    copy = pltpu.make_async_copy(held, out_ref, sent.at[0])
    copy.start()
    copy.wait()


def finished(known, arrived, scale):
    return pl.pallas_call(
        functools.partial(finished_kernel, scale),
        out_shape=jax.ShapeDtypeStruct(known.shape, known.dtype),
        in_specs=[VMEM, VMEM],
        out_specs=ANY,
        scratch_shapes=[pltpu.VMEM(known.shape, known.dtype), pltpu.SemaphoreType.DMA((1,))],
        compiler_params=params(),
        cost_estimate=cost(3 * known.size, 10 * known.size),
    )(known, arrived)


def per_device(cluster_maps, inverse_maps, seed_columns, seed_rows, ising_field, hop_bonds):
    clusters = lax.axis_size("tm")
    anchor = lax.axis_index("tm")
    ref_rows, sites = seed_columns.shape[1:]
    cores = lax.axis_size("col")
    core = lax.axis_index("col")

    def first_ref(displacement):
        origin = (core - (displacement > anchor).astype(jnp.int32)) % cores
        return (lax.axis_index("src") * cores + origin) * ref_rows

    def route(targets):
        return [
            (k * cores + c, t * cores + (c + shift) % cores)
            for k, (t, shift) in targets.items()
            for c in range(cores)
        ]

    around = route({k: ((k + 1) % clusters, (k + 1) // clusters) for k in range(clusters)})
    forward_map, inverse_map = turned(cluster_maps[0]), inverse_maps[0]
    first = first_ref(0)[None]
    forward_low, partner_low, forward, partner = packed(first, seed_columns[0], seed_rows[0])
    start = (forward, partner)

    terms = []
    for displacement in range(1, clusters):
        low = jnp.concatenate([forward_low, partner_low])
        if displacement >= 3:
            low, *terms[: displacement - 1] = lax.optimization_barrier((low, *terms[: displacement - 1]))
        low = lax.ppermute(low, ("tm", "col"), around)
        forward = jnp.dot(low[:ref_rows], forward_map, preferred_element_type=jnp.float32)
        partner = jnp.dot(low[ref_rows:], inverse_map, preferred_element_type=jnp.float32)
        forward_low, partner_low = forward.astype(jnp.bfloat16), partner.astype(jnp.bfloat16)
        if displacement == 1:
            field, bonds, *start = lax.optimization_barrier((ising_field[0], hop_bonds, *start, forward_low))[:4]
            rates = factors(field, bonds)
            terms.append(measured(first, *start, rates))
        terms.append(measured(first_ref(displacement)[None], forward, partner, rates))
    last = clusters - 1
    *early, late = terms
    early = jnp.stack(early)

    def early_term(target):
        return lax.dynamic_index_in_dim(early, jnp.minimum(target, last - 1), 0, keepdims=False)

    def sent(term, targets):
        return lax.ppermute(term, ("tm", "col"), route(targets))

    def shifted(step):
        return {k: ((k + step) % clusters, -(k < (k + step) % clusters)) for k in range(clusters)}

    arrived = [sent(early_term((anchor + step) % clusters), shifted(step)) for step in range(clusters - 2, 0, -1)]
    soon = sum(term.astype(jnp.float32) for term in arrived)

    total = jnp.where(anchor == last, late, early_term(anchor)).astype(jnp.float32)
    total = total + jnp.where(anchor == last, 0.0, soon)
    behind = jnp.where(anchor == 0, late, early_term(anchor - 1))
    soonest = jnp.where(anchor == 1, late, early_term(anchor))
    soonest, behind, late = lax.optimization_barrier((soonest, behind, late))

    def sent_last(term, k):
        swap = {m: (m, 1) for m in range(clusters)}
        term = sent(term, {**swap, k: (last, -1), last: (k, 1)})
        return jnp.where(anchor == last, term, 0.0).astype(jnp.float32)

    for k in range(last - 1, 1, -1):
        total = total + sent_last(late, k)
    total = total + sent_last(soonest, 1)
    arrived = sent(behind, shifted(-1))
    return finished(total, arrived, sites / clusters)[None]


def solution(mesh):
    in_specs = (
        P("tm", "chain", None),
        P("tm", "chain", None),
        P("tm", ("src", "col"), "chain"),
        P("tm", ("src", "col"), "chain"),
        P("tm", "chain", None),
        P(),
    )
    out_specs = P("tm", ("src", "col"), "chain")
    return jax.shard_map(
        per_device, mesh=mesh, in_specs=in_specs, out_specs=out_specs, check_vma=False
    )
```

```python
import functools
import math

import jax
import jax.numpy as jnp
from jax import lax
from jax.experimental import pallas as pl
from jax.experimental.pallas import tpu as pltpu
from jax.sharding import PartitionSpec as P

time_step = 0.25
field_coupling = math.log(math.exp(0.5) + math.sqrt(math.exp(1.0) - 1.0))

LANES = 128
SUBLANES = 8
VMEM = pl.BlockSpec(memory_space=pltpu.VMEM)
SMEM = pl.BlockSpec(memory_space=pltpu.SMEM)
ANY = pl.BlockSpec(memory_space=pl.ANY)


def params(mebibytes=4):
    return pltpu.CompilerParams(vmem_limit_bytes=mebibytes << 20)


def cost(flops, bytes_accessed):
    return pl.CostEstimate(flops=flops, bytes_accessed=bytes_accessed, transcendentals=0)


def rolled(blocks, shift):
    return [pltpu.roll(block, shift % LANES, 1) for block in blocks]


def split(values):
    return [values[:, j : j + LANES] for j in range(0, values.shape[1], LANES)]


def leads(blocks, side):
    return rolled(blocks, -side), rolled(blocks, side)


def beside(blocks, rows, side):
    column = lax.broadcasted_iota(jnp.int32, blocks[0].shape, 1) % side
    ahead, behind = rows
    right = [jnp.where(column == 0, q, u) for q, u in zip(behind, blocks)]
    left = [jnp.where(column == side - 1, q, u) for q, u in zip(ahead, blocks)]
    return rolled(right, -1), rolled(left, 1)


def hops(rows, columns, side, coefs):
    (ahead, behind), (right, left) = rows, columns
    count = len(ahead)
    lane = lax.broadcasted_iota(jnp.int32, ahead[0].shape, 1)
    out = []
    for j in range(count):
        row_ahead = jnp.where(lane < LANES - side, ahead[j], ahead[(j + 1) % count])
        row_behind = jnp.where(lane >= side, behind[j], behind[j - 1])
        up, down, forth, back = [c[j] for c in coefs]
        out.append((up * row_ahead + down * row_behind) + (forth * right[j] + back * left[j]))
    return out


def factors_kernel(side, field_ref, bonds_ref, out_ref):
    weights = bonds_ref[...].astype(jnp.float32) * time_step
    rows, columns = split(weights[0:1]), split(weights[1:2])
    lane = lax.broadcasted_iota(jnp.int32, rows[0].shape, 1)
    moved = rolled(rows, side)
    wrapped, left = rolled(columns, 1 - side), rolled(columns, 1)
    for j in range(len(rows)):
        place = slice(j * LANES, (j + 1) * LANES)
        out_ref[0:1, place] = rows[j]
        out_ref[1:2, place] = jnp.where(lane >= side, moved[j], moved[j - 1])
        out_ref[2:3, place] = columns[j]
        out_ref[3:4, place] = jnp.where(lane % side == 0, wrapped[j], left[j])
    spins = (2 * field_ref[...] - 1).astype(jnp.float32)
    wraps = spins.shape[0]
    out_ref[4 : 4 + wraps, :] = jnp.exp(field_coupling * spins)
    out_ref[4 + wraps : 4 + 2 * wraps, :] = jnp.exp(-field_coupling * spins)


def factors(field, bonds):
    wraps, sites = field.shape
    return pl.pallas_call(
        functools.partial(factors_kernel, math.isqrt(sites)),
        out_shape=jax.ShapeDtypeStruct((4 + 2 * wraps, sites), jnp.float32),
        in_specs=[VMEM, VMEM],
        out_specs=VMEM,
        compiler_params=params(),
        cost_estimate=cost(64 * sites, 64 * sites),
    )(field, bonds)


def measure_kernel(side, base_ref, forward_ref, partner_ref, factors_ref, out_ref):
    total = forward_ref.shape[0]
    count = SUBLANES if total % SUBLANES == 0 else total
    wraps = (factors_ref.shape[0] - 4) // 2
    coefs = [split(factors_ref[k : k + 1, :]) for k in range(4)]
    halves = [[0.5 * c for c in blocks] for blocks in coefs]
    groups = range(0, total, count)
    chains = [(ref, row, sign, place) for row in groups for ref, sign, place in ((forward_ref, 1.0, 4), (partner_ref, -1.0, 4 + wraps))]
    values = [split(ref[row : row + count, :]) for ref, row, _, _ in chains]
    for wrap in range(wraps):
        scales = {place: split(factors_ref[place + wrap : place + wrap + 1, :]) for place in (4, 4 + wraps)}
        values = [[u * s for u, s in zip(v, scales[place])] for v, (_, _, _, place) in zip(values, chains)]
        inner = values
        for weights in (halves, coefs):
            rows = [leads(v, side) for v in inner]
            columns = [beside(v, r, side) for v, r in zip(inner, rows)]
            inner = [
                [u + h if sign > 0 else u - h for u, h in zip(v, hops(r, c, side, weights))]
                for v, r, c, (_, _, sign, _) in zip(values, rows, columns, chains)
            ]
        values = inner
    row = lax.broadcasted_iota(jnp.int32, (total, LANES), 0) + base_ref[0]
    lane = lax.broadcasted_iota(jnp.int32, (total, LANES), 1)
    for j in range(len(coefs[0])):
        products = [f[j] * p[j] for f, p in zip(values[0::2], values[1::2])]
        term = jnp.where(lane + j * LANES == row, 0.0, jnp.concatenate(products))
        out_ref[:, j * LANES : (j + 1) * LANES] = term.astype(out_ref.dtype)


def measured(base, forward, partner, rates):
    return pl.pallas_call(
        functools.partial(measure_kernel, math.isqrt(forward.shape[1])),
        out_shape=jax.ShapeDtypeStruct(forward.shape, jnp.bfloat16),
        in_specs=[SMEM, VMEM, VMEM, VMEM],
        out_specs=VMEM,
        compiler_params=params(),
        cost_estimate=cost(45000 * forward.size, 12 * forward.size),
    )(base, forward, partner, rates)


def packed_kernel(base_ref, columns_ref, rows_ref, forward_low, partner_low, forward_ref, partner_ref, rows, arrived):
    copies = [
        pltpu.make_async_copy(columns_ref, forward_ref, arrived.at[0]),
        pltpu.make_async_copy(rows_ref, rows, arrived.at[1]),
    ]
    for copy in copies:
        copy.start()
    for copy in copies:
        copy.wait()
    row = lax.broadcasted_iota(jnp.int32, rows.shape, 0) + base_ref[0]
    lane = lax.broadcasted_iota(jnp.int32, rows.shape, 1)
    partner = jnp.where(lane == row, rows[...] - 1.0, rows[...])
    partner_ref[...] = partner
    partner_low[...] = partner.astype(partner_low.dtype)
    forward_low[...] = forward_ref[...].astype(forward_low.dtype)


def packed(base, columns, rows):
    low = jax.ShapeDtypeStruct(rows.shape, jnp.bfloat16)
    full = jax.ShapeDtypeStruct(rows.shape, jnp.float32)
    return pl.pallas_call(
        packed_kernel,
        out_shape=(low, low, full, full),
        in_specs=[SMEM, ANY, ANY],
        out_specs=(VMEM,) * 4,
        scratch_shapes=[pltpu.VMEM(rows.shape, rows.dtype), pltpu.SemaphoreType.DMA((2,))],
        compiler_params=params(),
        cost_estimate=cost(4 * rows.size, 12 * rows.size),
    )(
        base,
        pltpu.with_memory_space_constraint(columns, pltpu.HBM),
        pltpu.with_memory_space_constraint(rows, pltpu.HBM),
    )


def turned_kernel(map_ref, out_ref, held, arrived):
    rows = held.shape[1]
    copies = [
        pltpu.make_async_copy(map_ref.at[pl.ds(part * rows, rows)], held.at[part], arrived.at[part])
        for part in range(held.shape[0])
    ]
    for copy in copies:
        copy.start()
    for part, copy in enumerate(copies):
        copy.wait()
        out_ref[:, part * rows : (part + 1) * rows] = held[part].T


def turned(dense):
    parts = 4
    rows, columns = dense.shape[0] // parts, dense.shape[1]
    return pl.pallas_call(
        turned_kernel,
        out_shape=jax.ShapeDtypeStruct(dense.shape[::-1], dense.dtype),
        in_specs=[ANY],
        out_specs=VMEM,
        scratch_shapes=[pltpu.VMEM((parts, rows, columns), dense.dtype), pltpu.SemaphoreType.DMA((parts,))],
        compiler_params=params(8),
        cost_estimate=cost(dense.size, 4 * dense.size),
    )(pltpu.with_memory_space_constraint(dense, pltpu.HBM))


def per_device(cluster_maps, inverse_maps, seed_columns, seed_rows, ising_field, hop_bonds):
    clusters = lax.axis_size("tm")
    anchor = lax.axis_index("tm")
    ref_rows, sites = seed_columns.shape[1:]
    cores = lax.axis_size("col")
    core = lax.axis_index("col")

    def first_ref(displacement):
        origin = (core - (displacement > anchor).astype(jnp.int32)) % cores
        return (lax.axis_index("src") * cores + origin) * ref_rows

    def route(targets):
        return [
            (k * cores + c, t * cores + (c + shift) % cores)
            for k, (t, shift) in targets.items()
            for c in range(cores)
        ]

    around = route({k: ((k + 1) % clusters, (k + 1) // clusters) for k in range(clusters)})
    forward_map, inverse_map = turned(cluster_maps[0]), inverse_maps[0]
    first = first_ref(0)[None]
    forward_low, partner_low, forward, partner = packed(first, seed_columns[0], seed_rows[0])
    start = (forward, partner)

    terms = []
    for displacement in range(1, clusters):
        low = jnp.concatenate([forward_low, partner_low])
        if displacement >= 3:
            low, *terms[: displacement - 1] = lax.optimization_barrier((low, *terms[: displacement - 1]))
        low = lax.ppermute(low, ("tm", "col"), around)
        forward = jnp.dot(low[:ref_rows], forward_map, preferred_element_type=jnp.float32)
        partner = jnp.dot(low[ref_rows:], inverse_map, preferred_element_type=jnp.float32)
        forward_low, partner_low = forward.astype(jnp.bfloat16), partner.astype(jnp.bfloat16)
        if displacement == 1:
            field, bonds, *start = lax.optimization_barrier((ising_field[0], hop_bonds, *start, forward_low))[:4]
            rates = factors(field, bonds)
            terms.append(measured(first, *start, rates))
        terms.append(measured(first_ref(displacement)[None], forward, partner, rates))
    last = clusters - 1
    *early, late = terms
    early = jnp.stack(early)

    def early_term(target):
        return lax.dynamic_index_in_dim(early, jnp.minimum(target, last - 1), 0, keepdims=False)

    def sent(term, targets):
        return lax.ppermute(term, ("tm", "col"), route(targets))

    def shifted(step):
        return {k: ((k + step) % clusters, -(k < (k + step) % clusters)) for k in range(clusters)}

    arrived = [sent(early_term((anchor + step) % clusters), shifted(step)) for step in range(1, last)]
    soon = sum(term.astype(jnp.float32) for term in arrived)

    total = jnp.where(anchor == last, late, early_term(anchor)).astype(jnp.float32)
    total = total + jnp.where(anchor == last, 0.0, soon)
    behind = jnp.where(anchor == 0, late, early_term(anchor - 1))
    soonest = jnp.where(anchor == 1, late, early_term(anchor))
    soonest, behind, late = lax.optimization_barrier((soonest, behind, late))

    def sent_last(term, k):
        swap = {m: (m, 1) for m in range(clusters)}
        term = sent(term, {**swap, k: (last, -1), last: (k, 1)})
        return jnp.where(anchor == last, term, 0.0).astype(jnp.float32)

    total = total + sent_last(soonest, 1)
    for k in range(last - 1, 1, -1):
        total = total + sent_last(late, k)
    total = total + sent(behind, shifted(-1)).astype(jnp.float32)
    return (total * (sites / clusters))[None]


def solution(mesh):
    in_specs = (
        P("tm", "chain", None),
        P("tm", "chain", None),
        P("tm", ("src", "col"), "chain"),
        P("tm", ("src", "col"), "chain"),
        P("tm", "chain", None),
        P(),
    )
    out_specs = P("tm", ("src", "col"), "chain")
    return jax.shard_map(
        per_device, mesh=mesh, in_specs=in_specs, out_specs=out_specs, check_vma=False
    )
```
